512 devices in a mesh: row: 32 (over x, y_lo, core), col: 16 (over y_hi, z).
Axes of the slice: x: 4, y: 8 (y_hi: 2, y_lo: 4; y = y_hi * 4 + y_lo), z: 8, core: 2. Of those that a mesh axis runs over, the one named last changes fastest.
Arguments:
- amps: bfloat16 [800, 800, 256], P('col', 'row'), may hold values from -6 to 6
- integral: bfloat16 [800, 800, 256], P('row', 'col'), may hold values from -0.078125 to 0.078125
- virt_irrep: int32 [8], replicated, may hold values from 0 to 7
- occ_irrep: int32 [64], replicated, may hold values from 0 to 7
Outputs:
- resid: float32 [800, 4, 3200], P('row', None, 'col')
The draws below stay inside these ranges and needn't reach their ends.
Inputs may be any that keep to these rules, and one draw needn't show every extreme that they name: `virt_irrep`: labels of the eight D2h irreducible representations. `occ_irrep`: labels of the eight D2h irreducible representations.
All inputs are finite; a program needn't handle non-finite values.
Results may differ from the reference program's by a relative error of at most 0.005.
Values may be sent and summed in bfloat16 or wider, within the bound.
A program may use at most 128 MiB of HBM per device.

```python
import math
import jax
import jax.numpy as jnp
import numpy as np
from jax import lax

NV = 800
NO = 64
OW = 4
VBLK = 100
NB = 8


def plant(drawn, own_key, smallest, high):
    extent = drawn.shape
    index_at = [jax.random.randint(jax.random.fold_in(own_key, axis), (), 0, extent[axis]) for axis in range(len(extent))]
    drawn = drawn.at[tuple(index_at)].set(smallest)
    longest = extent.index(max(extent))
    index_at[longest] = (index_at[longest] + 1) % extent[longest]
    return drawn.at[tuple(index_at)].set(high)


def level_of(rng, shape, split, smallest, high):
    def one(axis_at, shards_of):
        draws = jax.random.uniform(jax.random.fold_in(jax.random.fold_in(rng, 6), axis_at), (shards_of,), jnp.float32, smallest / len(split), high / len(split))
        return jnp.repeat(jnp.exp(draws), shape[axis_at] // shards_of).reshape((-1,) + (1,) * (len(shape) - axis_at - 1))

    factor_of = one(*split[0])
    for cut in split[1:]:
        factor_of = factor_of * one(*cut)
    return factor_of


def rank_bounds(number_of, slope):
    loads = [(1 << 20) // math.isqrt(grade ** slope) + 1 for grade in range(1, number_of + 1)]
    scale = 1 + sum(loads) // (1 << 30)
    return np.cumsum(np.array([max(1, weight // scale) for weight in loads]))


def ranked(rng, extent, count, skew):
    grid = rank_bounds(count, skew)
    ticket = jax.random.randint(jax.random.fold_in(rng, 1), extent, 0, int(grid[count - 1]))
    grade = jnp.searchsorted(jnp.asarray(grid, jnp.int32), ticket, side="right")
    return jax.random.permutation(jax.random.fold_in(rng, 2), count)[grade].astype(jnp.int32)


def centred(stream_key, dims, width, bound, split=(), kind=jnp.bfloat16):
    gain = level_of(stream_key, dims, split, -0.22, 0.18) if split else 1.0
    drawn = jax.random.normal(stream_key, dims, jnp.float32) * width * gain
    return jnp.minimum(jnp.maximum(drawn, -bound), bound).astype(kind)


def setup_inputs(seed: int = 0) -> dict:
    arg_keys = jax.random.split(jax.random.key(seed), 5)
    amps = centred(arg_keys[0], (NV, NV, OW * NO), 1.0, 6.0, ((0, 16), (1, 32)))
    integral = centred(arg_keys[1], (NV, NV, NO * OW), (NV * NO // 8) ** -0.5, 0.078125, ((0, 32), (1, 16)))
    virt_irrep = plant(jax.random.randint(arg_keys[2], (NB,), 0, 8), jax.random.fold_in(arg_keys[2], 1), 0, 7).astype(jnp.int32)
    occ_irrep = plant(ranked(arg_keys[3], (NO,), 8, 2), jax.random.fold_in(arg_keys[3], 3), 0, 7).astype(jnp.int32)
    return {"amps": amps, "integral": integral, "virt_irrep": virt_irrep, "occ_irrep": occ_irrep}


def reference(amps, integral, virt_irrep, occ_irrep):
    virt_label = virt_irrep[(jnp.arange(NV) // VBLK).astype(jnp.int32)]
    window_label = occ_irrep[:OW]
    amp_four = amps.reshape(NV, NV, OW, NO)
    amp_keep = jnp.bitwise_xor(
        jnp.bitwise_xor(virt_label[:, None, None, None], virt_label[None, :, None, None]),
        jnp.bitwise_xor(window_label[None, None, :, None], occ_irrep[None, None, None, :])) == 0
    amp_masked = jnp.where(amp_keep, amp_four, jnp.zeros_like(amp_four))
    int_four = integral.reshape(NV, NV, NO, OW)
    int_keep = jnp.bitwise_xor(
        jnp.bitwise_xor(virt_label[:, None, None, None], virt_label[None, :, None, None]),
        jnp.bitwise_xor(occ_irrep[None, None, :, None], window_label[None, None, None, :])) == 0
    int_masked = jnp.where(int_keep, int_four, jnp.zeros_like(int_four))
    cycle = lax.dot_general(amp_masked.astype(jnp.float32), int_masked.astype(jnp.float32),
                           (((1, 3), (0, 2)), ((), ())))
    pair = (cycle - cycle.transpose(0, 3, 2, 1)).astype(jnp.bfloat16)
    pair_wide = pair.astype(jnp.float32)
    resid = pair_wide - pair_wide.transpose(2, 1, 0, 3)
    return resid.reshape(NV, OW, NV * OW)
```

```python
import functools

import jax
import jax.numpy as jnp
from jax import lax
from jax.experimental import pallas as pl
from jax.experimental.pallas import tpu as pltpu
from jax.sharding import PartitionSpec as P

MESH = pl.DeviceIdType.MESH
F32 = jnp.float32
BF16 = jnp.bfloat16
I32 = jnp.int32

NP = 50
NQ = 25
OW = 4
NO = 64
PAIRS = ((0, 1), (0, 2), (0, 3), (1, 2), (1, 3), (2, 3))
ROWS = 208
CUT = 112
SLOT = 64
MSG = len(PAIRS) * SLOT
ZN = 8
YH = 2


def iota(shape, dim):
    return lax.broadcasted_iota(I32, shape, dim)


def dot(a, b, dims):
    return lax.dot_general(a, b, (dims, ((), ())), preferred_element_type=F32)


NN = ((1,), (0,))
NT = ((1,), (1,))
TN = ((0,), (0,))


def kernel(cap, amps, integral, occ_row, occ, virt, out, ta, t32, tg, wall, st, sw, c32, keep, psend, precv, msg, p2r,
           zmat, tile, p3r, ag_s, ag_r, w_s, w_r, d_s, d_r, p2_s, p2_rs, p3_s, p3_rs, loc):
    group = 128 // cap
    tiles = -(-NQ // group)
    row = lax.axis_index("row")
    col = lax.axis_index("col")
    core = row % 2
    chip = row // 2
    yh = col // ZN
    z = col % ZN

    bar = pltpu.get_barrier_semaphore()

    def signal(r, c):
        pl.semaphore_signal(bar, inc=1, device_id=(r, c), device_id_type=MESH)

    right = yh * ZN + (z + 1) % ZN
    left = yh * ZN + (z + ZN - 1) % ZN
    opposite = (1 - yh) * ZN + z
    mate = row + 1 - 2 * core
    signal(row, right)
    signal(row, left)
    signal(row, opposite)
    signal(mate, col)
    home = chip // ZN

    def greet(n, carry):
        @pl.when(jnp.logical_not((n == chip) & (home == yh)))
        def _():
            signal(2 * n + core, home * ZN + z)

        return carry

    lax.fori_loop(0, 16, greet, 0)
    mirror_col = row // 2
    for s in range(2):
        @pl.when(jnp.logical_not((2 * col + s == row) & (mirror_col == col)))
        def _():
            signal(2 * col + s, mirror_col)

    own_p2 = (home == yh).astype(I32)
    own_p3 = (mirror_col == col).astype(I32)

    block_label = virt[col // 2] ^ virt[row // 4]
    lab = occ_row[...].astype(F32)
    wide = (256, NO)
    r256, l64 = iota(wide, 0), iota(wide, 1)

    def column(which):
        return jnp.sum(jnp.where(l64 == which, lab, 0.0), axis=1, keepdims=True)

    lane = iota((1, group * 128 * 4 // group), 1)
    lane_slot = lane % 128
    lane_key = (lane // 128) * 128 + lane_slot % cap
    lane_group = lane_slot // cap

    def select(ref, k_of, i_of):
        hk = column(k_of)
        hi = column(i_of)
        keep_it = (hk.astype(I32) ^ hi.astype(I32)) == block_label
        if cap == NO:
            place = k_of[:, :1]
        else:
            same = (lab == hk) & (l64 < k_of)
            place = jnp.sum(jnp.where(same, 1.0, 0.0), axis=1, keepdims=True).astype(I32)
        key = jnp.where(keep_it, i_of[:, :1] * 128 + place, -1)
        for g in range(group):
            hit = (key == lane_key) & (lane_group == g)
            ref[g * 256:(g + 1) * 256, :] = jnp.where(hit, 1.0, 0.0).astype(BF16)

    select(st, r256 % NO, r256 // NO)

    def widen(a, carry):
        plane = amps[a].astype(F32)
        for u in range(2):
            ta[u, pl.ds(pl.multiple_of(a * 32, 32), NQ), :] = plane[:, u * 128:(u + 1) * 128]
        return carry

    lax.fori_loop(0, NP, widen, 0, unroll=5)
    t32[OW * NP:ROWS, :] = jnp.zeros((ROWS - OW * NP, tiles * 128), F32)
    for q in range(tiles):
        cs = range(q * group, min(NQ, (q + 1) * group))
        x = jnp.concatenate([ta[u, pl.ds(c, NP, stride=32), :].astype(BF16) for c in cs for u in range(2)], axis=1)
        y = dot(x, st[0:len(cs) * 256, :], NN)
        for i in range(OW):
            t32[i * NP:(i + 1) * NP, q * 128:(q + 1) * 128] = y[:, i * 128:(i + 1) * 128]
    tg[z] = t32[...].astype(BF16)

    pl.semaphore_wait(bar, 22 - own_p2 - own_p3)

    parts = ((0, CUT), (CUT, ROWS - CUT))

    def hop(direction, step, part):
        src = (z + ZN - step) % ZN if direction == 0 else (z + step) % ZN
        lo, size = parts[part]
        n = (direction * 4 + step) * 2 + part
        return pltpu.make_async_remote_copy(
            src_ref=tg.at[src, pl.ds(lo, size)], dst_ref=tg.at[src, pl.ds(lo, size)], send_sem=ag_s.at[n], recv_sem=ag_r.at[n],
            device_id=(row, right if direction == 0 else left), device_id_type=MESH)

    def arrival(direction, step, part):
        src = (z + ZN - step - 1) % ZN if direction == 0 else (z + step + 1) % ZN
        lo, size = parts[part]
        n = (direction * 4 + step) * 2 + part
        return pltpu.make_async_remote_copy(
            src_ref=tg.at[src, pl.ds(lo, size)], dst_ref=tg.at[src, pl.ds(lo, size)], send_sem=ag_s.at[n], recv_sem=ag_r.at[n],
            device_id=(row, right if direction == 0 else left), device_id_type=MESH)

    for part in range(2):
        for d in range(2):
            hop(d, 0, part).start()

    select(sw, r256 // OW, r256 % OW)
    for q in range(tiles):
        cs = range(q * group, min(NQ, (q + 1) * group))
        x = jnp.concatenate([integral[c] for c in cs], axis=1)
        y = dot(x, sw[0:len(cs) * 256, :], NN)
        y = jnp.concatenate([y, jnp.zeros((SLOT - NP, 512), F32)], axis=0).astype(BF16)
        for j in range(OW):
            wall[yh, j * SLOT:(j + 1) * SLOT, q * 128:(q + 1) * 128] = y[:, j * 128:(j + 1) * 128]
    swap = pltpu.make_async_remote_copy(
        src_ref=wall.at[yh], dst_ref=wall.at[yh], send_sem=w_s, recv_sem=w_r, device_id=(row, opposite), device_id_type=MESH)
    swap_in = pltpu.make_async_remote_copy(
        src_ref=wall.at[1 - yh], dst_ref=wall.at[1 - yh], send_sem=w_s, recv_sem=w_r, device_id=(row, opposite), device_id_type=MESH)
    swap.start()

    zr, zl = iota((MSG, OW * 256), 0), iota((MSG, OW * 256), 1)
    zp, zb = zr // SLOT, zr % SLOT
    zi, zt = zl // 256, zl % 256
    first = jnp.where(zp < 3, 0, jnp.where(zp < 5, 1, 2))
    second = jnp.where(zp < 3, zp + 1, jnp.where(zp < 5, zp - 1, 3))
    here = (zt // OW == zb) & (zb < NP)
    plus = here & (zi == first) & (zt % OW == second)
    minus = here & (zi == second) & (zt % OW == first)
    zmat[...] = (jnp.where(plus, 1.0, 0.0) - jnp.where(minus, 1.0, 0.0)).astype(BF16)

    low = iota((32, 128), 1) < SLOT

    def mate_copy(n):
        return pltpu.make_async_remote_copy(
            src_ref=psend.at[n], dst_ref=precv.at[n], send_sem=d_s.at[n], recv_sem=d_r.at[n], device_id=(mate, col),
            device_id_type=MESH)

    def compute(n, off):
        za = (z + off) % ZN
        for h in range(YH):
            c32[:, h * 256:(h + 1) * 256] = dot(tg[za], wall[h], NT)
        la = virt[(yh * ZN + za) // 2]
        halves = []
        for half in range(2):
            line = []
            for h in range(YH):
                lb = virt[(h * ZN + z) // 2]
                for t in range(3):
                    both = []
                    for p in (2 * t, 2 * t + 1):
                        i, j = PAIRS[p]

                        def piece(r, s):
                            start = NP * r + NQ * half
                            v = c32[start:start + 32, h * 256 + (s // 2) * 128:h * 256 + (s // 2) * 128 + 128]
                            return v if s % 2 == p % 2 else pltpu.roll(v, SLOT, axis=1)

                        scale = jnp.where((la ^ lb ^ occ[i] ^ occ[j]) == 0, 1.0, 0.0)
                        both.append((piece(i, j) - piece(j, i)) * scale)
                    line.append(jnp.where(low, both[0], both[1]))
            halves.append(jnp.concatenate(line, axis=1))
        keep[n] = jnp.where(core == 0, halves[0], halves[1])
        psend[n] = jnp.where(core == 0, halves[1], halves[0]).astype(BF16)
        mate_copy(n).start()

    def finish(n, off):
        za = (z + off) % ZN
        mate_copy(n).wait_recv()
        total = (keep[n] + precv[n].astype(F32)).astype(BF16)
        for h in range(YH):
            msg[n, h] = total[:, h * MSG:(h + 1) * MSG]
            to_row = 2 * (yh * ZN + za) + core
            mine = (to_row == row) & (yh == h)

            @pl.when(jnp.logical_not(mine))
            def _():
                pltpu.make_async_remote_copy(
                    src_ref=msg.at[n, h], dst_ref=p2r.at[chip], send_sem=p2_s, recv_sem=p2_rs,
                    device_id=(to_row, h * ZN + z), device_id_type=MESH).start()

            @pl.when(mine)
            def _():
                pltpu.make_async_copy(msg.at[n, h], p2r.at[chip], p2_rs).start()

    order = (0, ZN - 1, 1, ZN - 2, 2, ZN - 3, 3, 4)
    for step in range(1, 4):
        for part in range(2):
            for d in range(2):
                arrival(d, step - 1, part).wait_recv()
                if step < 3 or part == d:
                    hop(d, step, part).start()
        if step == 2:
            swap_in.wait_recv()
            for n in range(5):
                compute(n, order[n])
            for n in range(5):
                finish(n, order[n])
        if step == 3:
            for n in (5, 6):
                compute(n, order[n])
            for n in (5, 6):
                finish(n, order[n])
    for d in range(2):
        arrival(d, 3, d).wait_recv()
    compute(7, order[7])
    finish(7, order[7])

    pltpu.make_async_copy(p2r, p2r, p2_rs).wait()
    total = p2r[0].astype(F32)
    for n in range(1, 16):
        total = total + p2r[n].astype(F32)
    tile[...] = total.astype(BF16)

    def mirror_copy(s):
        return pltpu.make_async_remote_copy(
            src_ref=tile, dst_ref=p3r.at[row % 2], send_sem=p3_s.at[s], recv_sem=p3_rs.at[row % 2],
            device_id=(2 * col + s, mirror_col), device_id_type=MESH)

    for s in range(2):
        self_mirror = (2 * col + s == row) & (mirror_col == col)

        @pl.when(jnp.logical_not(self_mirror))
        def _():
            mirror_copy(s).start()

        @pl.when(self_mirror)
        def _():
            pltpu.make_async_copy(tile, p3r.at[s], p3_rs.at[s]).start()

    base = dot(tile[...], zmat[...], NN)
    er, el = iota((32, 256), 0), iota((32, 256), 1)
    spread = None
    for s in range(2):
        pltpu.make_async_copy(p3r.at[s], p3r.at[s], p3_rs.at[s]).wait()
        put = ((el % 128) == er + NQ * s + SLOT * (el // 128)) & (er < NQ)
        part = dot(p3r[s], jnp.where(put, 1.0, 0.0).astype(BF16), TN)
        spread = part if spread is None else spread + part
    line = []
    for t in range(3):
        both = []
        for u in range(2):
            lo = (2 * t + u) * SLOT
            a0 = spread[lo:lo + 32, u * 128:(u + 1) * 128]
            a1 = spread[lo + NQ:lo + NQ + 32, u * 128:(u + 1) * 128]
            both.append(jnp.where(row % 2 == 0, a0, a1))
        line.append(both[0] + both[1])
    swapped = jnp.concatenate(line, axis=1).astype(BF16)
    res = base - dot(swapped, zmat[...], NN)
    for i in range(OW):
        out[i] = res[0:NQ, i * 256:i * 256 + NP * OW]

    for part in range(2):
        for d in range(2):
            for step in range(4):
                if step < 3 or part == d:
                    hop(d, step, part).wait_send()
    swap.wait_send()
    for n in range(8):
        mate_copy(n).wait_send()

    @pl.when(home == yh)
    def _():
        pltpu.make_async_copy(p2r.at[pl.ds(0, 15)], p2r.at[pl.ds(0, 15)], p2_s).wait()

    @pl.when(home != yh)
    def _():
        pltpu.make_async_copy(p2r, p2r, p2_s).wait()

    for s in range(2):
        @pl.when(jnp.logical_not((2 * col + s == row) & (mirror_col == col)))
        def _():
            mirror_copy(s).wait_send()


def call(cap, collective_id, amps, integral, virt_irrep, occ_irrep):
    group = 128 // cap
    lanes = -(-NQ // group) * 128
    vmem = pl.BlockSpec(memory_space=pltpu.VMEM)
    smem = pl.BlockSpec(memory_space=pltpu.SMEM)
    dma = pltpu.SemaphoreType.DMA
    return pl.pallas_call(
        functools.partial(kernel, cap),
        out_shape=jax.ShapeDtypeStruct((OW, NQ, NP * OW), F32),
        in_specs=[vmem, vmem, vmem, smem, smem],
        out_specs=vmem,
        scratch_shapes=[
            pltpu.VMEM((2, NP * 32, 128), F32),
            pltpu.VMEM((ROWS, lanes), F32),
            pltpu.VMEM((ZN, ROWS, lanes), BF16),
            pltpu.VMEM((YH, OW * SLOT, lanes), BF16),
            pltpu.VMEM((group * 256, 512), BF16),
            pltpu.VMEM((group * 256, 512), BF16),
            pltpu.VMEM((ROWS, 512), F32),
            pltpu.VMEM((ZN, 32, YH * MSG), F32),
            pltpu.VMEM((ZN, 32, YH * MSG), BF16),
            pltpu.VMEM((ZN, 32, YH * MSG), BF16),
            pltpu.VMEM((ZN, YH, 32, MSG), BF16),
            pltpu.VMEM((16, 32, MSG), BF16),
            pltpu.VMEM((MSG, OW * 256), BF16),
            pltpu.VMEM((32, MSG), BF16),
            pltpu.VMEM((2, 32, MSG), BF16),
            dma((16,)), dma((16,)), dma, dma, dma((ZN,)), dma((ZN,)), dma, dma, dma((2,)), dma((2,)), dma,
        ],
        name="cycle%d" % cap,
        compiler_params=pltpu.CompilerParams(
            collective_id=collective_id, has_side_effects=True, vmem_limit_bytes=48 * 2**20),
    )(amps, integral, occ_irrep.reshape(1, NO), occ_irrep, virt_irrep)


def shards(amps, integral, virt_irrep, occ_irrep):
    tile = call(NO, 0, amps, integral, virt_irrep, occ_irrep)
    return tile.transpose(1, 0, 2)


def solution(mesh):
    placed = (P("col", "row", None), P("row", "col", None), P(), P())
    return jax.shard_map(
        shards, mesh=mesh, in_specs=placed, out_specs=P("row", None, "col"), check_vma=False
    )
```

```python
import functools

import jax
import jax.numpy as jnp
from jax import lax
from jax.experimental import pallas as pl
from jax.experimental.pallas import tpu as pltpu
from jax.sharding import PartitionSpec as P

MESH = pl.DeviceIdType.MESH
F32 = jnp.float32
BF16 = jnp.bfloat16
I32 = jnp.int32

NP = 50
NQ = 25
OW = 4
NO = 64
PAIRS = ((0, 1), (0, 2), (0, 3), (1, 2), (1, 3), (2, 3))
SLOT = 64
MSG = len(PAIRS) * SLOT
ZN = 8
YH = 2


def iota(shape, dim):
    return lax.broadcasted_iota(I32, shape, dim)


def dot(a, b, dims):
    return lax.dot_general(a, b, (dims, ((), ())), preferred_element_type=F32)


class Plan:
    def __init__(self, lanes, cap):
        self.lanes, self.cap = lanes, cap
        self.group = 128 // cap
        self.full = NQ // self.group
        self.wide = self.group * lanes // 128
        self.last = -(-lanes // 128)
        self.span = self.full * self.wide + self.last
        self.rest = -(-2 * (self.full + 1) // 16)
        self.count = 3 * self.span + self.rest * self.wide
        self.depth = (self.full + 1) * 128


NN = ((1,), (0,))
NT = ((1,), (1,))
TN = ((0,), (0,))


def kernel(plan, amps, integral, occ_row, occ, virt, out, blk, wblk, rest32, st, sw, ex, y32, texp, wall, c32, keep, psend,
           precv, msg, p2r, zmat, tile, p3r, ag_s, ag_r, w_s, w_r, d_s, d_r, p2_s, p2_rs, p3_s, p3_rs, word):
    group, wide, span, full = plan.group, plan.wide, plan.span, plan.full
    dense = plan.lanes == OW * NO
    row = lax.axis_index("row")
    col = lax.axis_index("col")
    core = row % 2
    chip = row // 2
    yh = col // ZN
    z = col % ZN

    right = yh * ZN + (z + 1) % ZN
    left = yh * ZN + (z + ZN - 1) % ZN
    opposite = (1 - yh) * ZN + z
    mate = row + 1 - 2 * core
    home = chip // ZN
    home_z = chip % ZN
    late_owner = home_z == (z + 4) % ZN
    mirror_col = row // 2
    own_p2 = (home == yh).astype(I32)
    own_p3 = (mirror_col == col).astype(I32)

    x, y = row // 8, yh * 4 + chip % 4

    def at_x(d):
        return ((x + 4 + d) % 4 * 8 + row % 8, col)

    def at_y(d):
        to = (y + 8 + d) % 8
        return (x * 8 + to % 4 * 2 + core, to // 4 * ZN + z)

    def at_z(d):
        return (row, yh * ZN + (z + ZN + d) % ZN)

    bar = pltpu.get_barrier_semaphore()
    near = [at(d) for at in (at_x, at_y, at_z) for d in (1, -1)] + [(mate, col)]
    for to in near:
        pl.semaphore_signal(bar, inc=1, device_id=to, device_id_type=MESH)

    rounds = ((at_y, 2), (at_y, 2), (at_y, 1), (at_x, 2), (at_x, 1), (None, 1), (at_z, 2), (at_z, 2), (at_z, 2), (at_z, 1))

    def tell(n):
        at, ways = rounds[n]
        for way in range(ways):
            to = (mate, col) if at is None else at(1 - 2 * way)
            pl.semaphore_signal(word.at[2 * n + way], inc=1, device_id=to, device_id_type=MESH)

    def hear(n):
        for way in range(rounds[n][1]):
            pl.semaphore_wait(word.at[2 * n + way], 1)

    block_irrep = virt[row // 4]
    lab = occ_row[...]

    def offsets(label):
        counts = [jnp.sum(jnp.where(lab == (label ^ occ[i]), 1.0, 0.0), axis=1, keepdims=True).astype(I32) for i in range(OW)]
        if dense:
            return [jnp.full((1, 1), i * NO, I32) for i in range(OW)], [jnp.full((1, 1), NO, I32)] * OW
        return [sum(counts[:i], jnp.zeros((1, 1), I32)) for i in range(OW)], counts

    def by_window(which, values):
        return jnp.where(which == 0, values[0], jnp.where(which == 1, values[1], jnp.where(which == 2, values[2], values[3])))

    labf = lab.astype(F32)
    r256, l64 = iota((256, NO), 0), iota((256, NO), 1)
    here = virt[col // 2] ^ block_irrep
    here_off, _ = offsets(here)
    pl_lane = iota((1, group * plan.lanes), 1)

    def select(ref, k_of, i_of):
        hk = jnp.sum(jnp.where(l64 == k_of, labf, 0.0), axis=1, keepdims=True)
        k1, i1 = k_of[:, :1], i_of[:, :1]
        hi = by_window(i1, [occ[i] for i in range(OW)])
        if dense:
            place = k1
        else:
            same = (labf == hk) & (l64 < k_of)
            place = jnp.sum(jnp.where(same, 1.0, 0.0), axis=1, keepdims=True).astype(I32)
        key = jnp.where((hk.astype(I32) ^ hi) == here, by_window(i1, here_off) + place, -1)
        for g in range(group):
            hit = (key == pl_lane % plan.lanes) & (pl_lane // plan.lanes == g)
            ref[g * 256:(g + 1) * 256, :] = jnp.where(hit, 1.0, 0.0).astype(BF16)

    def pack(planes, sel, dst):
        for q in range(full + 1):
            cs = range(q * group, min(NQ, (q + 1) * group))
            many = wide if q < full else plan.last
            x = jnp.concatenate([planes[c] for c in cs], axis=1)
            y = dot(x, sel[0:len(cs) * 256, 0:many * 128], NN)
            for r in range(3):
                for t in range(many):
                    dst[r * span + q * wide + t] = y[r * 16:(r + 1) * 16, t * 128:(t + 1) * 128].astype(BF16)
            rest32[2 * q:2 * q + 2, 0:many * 128] = y[48:50, :]
        for r in range(plan.rest):
            for t in range(wide):
                dst[3 * span + r * wide + t] = rest32[r * 16:(r + 1) * 16, t * 128:(t + 1) * 128].astype(BF16)

    def expand(src, sel, dst):
        lines = [jnp.concatenate([src[r * span + q * wide + t] for t in range(wide)], axis=1)
                 for q in range(full) for r in range(3)]
        lines += [jnp.concatenate([src[3 * span + r * wide + t] for t in range(wide)], axis=1) for r in range(plan.rest)]
        tall = 48 * full
        y32[0:tall + 16 * plan.rest, :] = dot(jnp.concatenate(lines, axis=0), sel[...], NN)
        x = jnp.concatenate([jnp.concatenate([src[r * span + full * wide + t] for t in range(plan.last)], axis=1)
                             for r in range(3)], axis=0)
        z6 = dot(x, sel[0:plan.last * 128, :], NN)
        for q in range(full + 1):
            for i in range(OW):
                lanes = slice(i * 128, (i + 1) * 128)
                main = y32[q * 48:(q + 1) * 48, lanes] if q < full else z6[:, lanes]
                dst[i * SLOT:i * SLOT + 48, q * 128:(q + 1) * 128] = main.astype(BF16)
                dst[i * SLOT + 48:i * SLOT + 50, q * 128:(q + 1) * 128] = (
                    y32[tall + 2 * q:tall + 2 * q + 2, lanes].astype(BF16))

    rest32[...] = jnp.zeros(rest32.shape, F32)
    select(st, r256 % NO, r256 // NO)
    pack(amps, st, blk.at[z])

    pl.semaphore_wait(bar, len(near))

    cut = plan.count // 2
    parts = ((0, cut), (cut, plan.count - cut))

    def moved(direction, step, part, src):
        lo, size = parts[part]
        n = (direction * 4 + step) * 2 + part
        ref = blk.at[src, pl.ds(lo, size)]
        return pltpu.make_async_remote_copy(
            src_ref=ref, dst_ref=ref, send_sem=ag_s.at[n], recv_sem=ag_r.at[n],
            device_id=(row, right if direction == 0 else left), device_id_type=MESH)

    def hop(direction, step, part):
        return moved(direction, step, part, (z + ZN - step) % ZN if direction == 0 else (z + step) % ZN)

    def arrival(direction, step, part):
        return moved(direction, step, part, (z + ZN - step - 1) % ZN if direction == 0 else (z + step + 1) % ZN)

    for part in range(2):
        for d in range(2):
            hop(d, 0, part).start()

    tell(0)
    select(sw, r256 // OW, r256 % OW)
    hear(0)
    tell(1)
    pack(integral, sw, wblk.at[yh])
    hear(1)
    tell(2)

    def swap(which):
        return pltpu.make_async_remote_copy(
            src_ref=wblk.at[which], dst_ref=wblk.at[which], send_sem=w_s, recv_sem=w_r, device_id=(row, opposite),
            device_id_type=MESH)

    er = iota((group * plan.lanes, 1), 0)
    el = iota((1, 512), 1)
    e_i, e_g, e_m = el // 128, (el % 128) // plan.cap, el % plan.cap
    for n in range(5):
        label = block_irrep ^ (virt[yh * 4 + n] if n < 4 else virt[(1 - yh) * 4 + z // 2])
        off, counts = offsets(label)
        key = jnp.where(e_m < by_window(e_i, counts), by_window(e_i, off) + e_m, -1)
        hit = (er % plan.lanes == key) & (er // plan.lanes == e_g)
        ex[n] = jnp.where(hit, 1.0, 0.0).astype(BF16)

    hear(2)
    swap(yh).start()
    tell(3)
    texp[...] = jnp.zeros(texp.shape, BF16)
    wall[...] = jnp.zeros(wall.shape, BF16)
    hear(3)
    tell(4)

    zr, zl = iota((MSG, OW * 256), 0), iota((MSG, OW * 256), 1)
    zp, zb = zr // SLOT, zr % SLOT
    zi, zt = zl // 256, zl % 256
    first = jnp.where(zp < 3, 0, jnp.where(zp < 5, 1, 2))
    second = jnp.where(zp < 3, zp + 1, jnp.where(zp < 5, zp - 1, 3))
    in_b = (zt // OW == zb) & (zb < NP)
    plus = in_b & (zi == first) & (zt % OW == second)
    minus = in_b & (zi == second) & (zt % OW == first)
    zmat[...] = (jnp.where(plus, 1.0, 0.0) - jnp.where(minus, 1.0, 0.0)).astype(BF16)

    low = iota((32, 128), 1) < SLOT
    order = (0, ZN - 1, 1, ZN - 2, 2, ZN - 3, 3, 4)

    def unpack(n):
        za = (z + order[n]) % ZN
        expand(blk.at[za], ex.at[za // 2], texp.at[n])

    def mate_copy(n):
        return pltpu.make_async_remote_copy(
            src_ref=psend.at[n], dst_ref=precv.at[n], send_sem=d_s.at[n], recv_sem=d_r.at[n], device_id=(mate, col),
            device_id_type=MESH)

    def differences(n):
        za = (z + order[n]) % ZN
        for h in range(YH):
            c32[:, h * 256:(h + 1) * 256] = dot(texp[n], wall[h], NT)
        la = virt[(yh * ZN + za) // 2]
        halves = []
        for half in range(2):
            line = []
            for h in range(YH):
                lb = virt[(h * ZN + z) // 2]
                for t in range(3):
                    both = []
                    for p in (2 * t, 2 * t + 1):
                        i, j = PAIRS[p]

                        def piece(r, s):
                            start = SLOT * r + NQ * half
                            v = c32[start:start + 32, h * 256 + (s // 2) * 128:h * 256 + (s // 2) * 128 + 128]
                            return v if s % 2 == p % 2 else pltpu.roll(v, SLOT, axis=1)

                        scale = jnp.where((la ^ lb ^ occ[i] ^ occ[j]) == 0, 1.0, 0.0)
                        both.append((piece(i, j) - piece(j, i)) * scale)
                    line.append(jnp.where(low, both[0], both[1]))
            halves.append(jnp.concatenate(line, axis=1))
        return halves

    def compute(n):
        halves = differences(n)
        keep[n] = jnp.where(core == 0, halves[0], halves[1])
        psend[n] = jnp.where(core == 0, halves[1], halves[0]).astype(BF16)
        mate_copy(n).start()

    def deliver(m, to_row, h, place):
        mine = (to_row == row) & (yh == h)

        @pl.when(jnp.logical_not(mine))
        def _():
            pltpu.make_async_remote_copy(
                src_ref=msg.at[m], dst_ref=p2r.at[place], send_sem=p2_s, recv_sem=p2_rs,
                device_id=(to_row, h * ZN + z), device_id_type=MESH).start()

        @pl.when(mine)
        def _():
            pltpu.make_async_copy(msg.at[m], p2r.at[place], p2_rs).start()

    def finish(n):
        za = (z + order[n]) % ZN
        mate_copy(n).wait_recv()
        total = (keep[n] + precv[n].astype(F32)).astype(BF16)
        for h in range(YH):
            msg[2 * n + h] = total[:, h * MSG:(h + 1) * MSG]
            deliver(2 * n + h, 2 * (yh * ZN + za) + core, h, chip)

    def forward(step):
        for part in range(2):
            for d in range(2):
                arrival(d, step - 1, part).wait_recv()
                if step < 3 or part == d:
                    hop(d, step, part).start()

    hear(4)
    tell(5)
    expand(wblk.at[yh], ex.at[z // 2], wall.at[yh])
    unpack(0)
    hear(5)
    tell(6)
    forward(1)
    unpack(1)
    unpack(2)
    hear(6)
    tell(7)
    forward(2)
    unpack(3)
    unpack(4)
    hear(7)
    tell(8)
    swap(1 - yh).wait_recv()
    expand(wblk.at[1 - yh], ex.at[4], wall.at[1 - yh])
    compute(0)
    forward(3)
    hear(8)
    tell(9)
    for n in range(1, 5):
        compute(n)
    for n in (5, 6):
        unpack(n)
        compute(n)
    for n in range(7):
        finish(n)
    for d in range(2):
        arrival(d, 3, d).wait_recv()
    unpack(7)
    halves = differences(7)
    za = (z + order[7]) % ZN
    for half in range(2):
        total = halves[half].astype(BF16)
        for h in range(YH):
            m = 14 + 2 * half + h
            msg[m] = total[:, h * MSG:(h + 1) * MSG]
            deliver(m, 2 * (yh * ZN + za) + half, h, row)

    def add_up(many):
        pltpu.make_async_copy(p2r.at[pl.ds(0, many)], p2r.at[pl.ds(0, many)], p2_rs).wait()
        total = p2r[0].astype(F32)
        for n in range(1, many):
            total = total + p2r[n].astype(F32)
        tile[...] = total.astype(BF16)

    @pl.when(late_owner)
    def _():
        add_up(32)

    @pl.when(jnp.logical_not(late_owner))
    def _():
        add_up(16)

    hear(9)
    def mirror_copy(s):
        return pltpu.make_async_remote_copy(
            src_ref=tile, dst_ref=p3r.at[row % 2], send_sem=p3_s.at[s], recv_sem=p3_rs.at[row % 2],
            device_id=(2 * col + s, mirror_col), device_id_type=MESH)

    for s in range(2):
        self_mirror = (2 * col + s == row) & (mirror_col == col)

        @pl.when(jnp.logical_not(self_mirror))
        def _():
            mirror_copy(s).start()

        @pl.when(self_mirror)
        def _():
            pltpu.make_async_copy(tile, p3r.at[s], p3_rs.at[s]).start()

    base = dot(tile[...], zmat[...], NN)
    br, bl = iota((32, 256), 0), iota((32, 256), 1)
    spread = None
    for s in range(2):
        pltpu.make_async_copy(p3r.at[s], p3r.at[s], p3_rs.at[s]).wait()
        put = ((bl % 128) == br + NQ * s + SLOT * (bl // 128)) & (br < NQ)
        part = dot(p3r[s], jnp.where(put, 1.0, 0.0).astype(BF16), TN)
        spread = part if spread is None else spread + part
    line = []
    for t in range(3):
        both = []
        for u in range(2):
            lo = (2 * t + u) * SLOT
            a0 = spread[lo:lo + 32, u * 128:(u + 1) * 128]
            a1 = spread[lo + NQ:lo + NQ + 32, u * 128:(u + 1) * 128]
            both.append(jnp.where(row % 2 == 0, a0, a1))
        line.append(both[0] + both[1])
    swapped = jnp.concatenate(line, axis=1).astype(BF16)
    res = base - dot(swapped, zmat[...], NN)
    for i in range(OW):
        out[i] = res[0:NQ, i * 256:i * 256 + NP * OW]

    for part in range(2):
        for d in range(2):
            for step in range(4):
                if step < 3 or part == d:
                    hop(d, step, part).wait_send()
    swap(yh).wait_send()
    for n in range(7):
        mate_copy(n).wait_send()

    @pl.when(home == yh)
    def _():
        pltpu.make_async_copy(msg.at[pl.ds(0, 17)], msg.at[pl.ds(0, 17)], p2_s).wait()

    @pl.when(home != yh)
    def _():
        pltpu.make_async_copy(msg, msg, p2_s).wait()

    for s in range(2):
        @pl.when(jnp.logical_not((2 * col + s == row) & (mirror_col == col)))
        def _():
            mirror_copy(s).wait_send()


def call(lanes, cap, collective_id, amps, integral, virt_irrep, occ_irrep):
    plan = Plan(lanes, cap)
    vmem = pl.BlockSpec(memory_space=pltpu.VMEM)
    smem = pl.BlockSpec(memory_space=pltpu.SMEM)
    dma = pltpu.SemaphoreType.DMA
    return pl.pallas_call(
        functools.partial(kernel, plan),
        out_shape=jax.ShapeDtypeStruct((OW, NQ, NP * OW), F32),
        in_specs=[vmem, vmem, vmem, smem, smem],
        out_specs=vmem,
        scratch_shapes=[
            pltpu.VMEM((ZN, plan.count, 16, 128), BF16),
            pltpu.VMEM((YH, plan.count, 16, 128), BF16),
            pltpu.VMEM((plan.rest * 16, plan.wide * 128), F32),
            pltpu.VMEM((plan.group * 256, plan.wide * 128), BF16),
            pltpu.VMEM((plan.group * 256, plan.wide * 128), BF16),
            pltpu.VMEM((5, plan.wide * 128, 512), BF16),
            pltpu.VMEM((48 * plan.full + 16 * plan.rest, 512), F32),
            pltpu.VMEM((ZN, OW * SLOT, plan.depth), BF16),
            pltpu.VMEM((YH, OW * SLOT, plan.depth), BF16),
            pltpu.VMEM((OW * SLOT, 512), F32),
            pltpu.VMEM((ZN - 1, 32, YH * MSG), F32),
            pltpu.VMEM((ZN - 1, 32, YH * MSG), BF16),
            pltpu.VMEM((ZN - 1, 32, YH * MSG), BF16),
            pltpu.VMEM((18, 32, MSG), BF16),
            pltpu.VMEM((32, 32, MSG), BF16),
            pltpu.VMEM((MSG, OW * 256), BF16),
            pltpu.VMEM((32, MSG), BF16),
            pltpu.VMEM((2, 32, MSG), BF16),
            dma((16,)), dma((16,)), dma, dma, dma((ZN - 1,)), dma((ZN - 1,)), dma, dma, dma((2,)), dma((2,)),
            pltpu.SemaphoreType.REGULAR((20,)),
        ],
        name="cycle%d" % lanes,
        compiler_params=pltpu.CompilerParams(
            collective_id=collective_id, has_side_effects=True, vmem_limit_bytes=48 * 2**20),
    )(amps, integral, occ_irrep.reshape(1, NO), occ_irrep, virt_irrep)


TIERS = ((64, 32), (96, 32), (OW * NO, NO))


def shards(amps, integral, virt_irrep, occ_irrep):
    partner = jnp.concatenate([occ_irrep[:OW], jnp.zeros((1,), I32)])
    weight = jnp.array([1, 1, 1, 1, 1024], I32)
    hits = (occ_irrep[:, None, None] ^ partner[None, :, None]) == jnp.arange(8, dtype=I32)
    sums = jnp.sum(jnp.where(hits, weight[None, :, None], 0), axis=(0, 1))
    need = sums % 1024
    tier = jnp.max(jnp.where(sums // 1024 > 32, 2, (need > 64).astype(I32) + (need > 96).astype(I32)))
    calls = [functools.partial(call, lanes, cap, n) for n, (lanes, cap) in enumerate(TIERS)]
    tile = lax.switch(tier, calls, amps.transpose(1, 0, 2), integral, virt_irrep, occ_irrep)
    return tile.transpose(1, 0, 2)


def solution(mesh):
    placed = (P("col", "row", None), P("row", "col", None), P(), P())
    return jax.shard_map(
        shards, mesh=mesh, in_specs=placed, out_specs=P("row", None, "col"), check_vma=False
    )
```

```python
import functools

import jax
import jax.numpy as jnp
import numpy as np
from jax import lax
from jax.experimental import pallas as pl
from jax.experimental.pallas import tpu as pltpu
from jax.sharding import PartitionSpec as P

MESH = pl.DeviceIdType.MESH
F32 = jnp.float32
BF16 = jnp.bfloat16
I32 = jnp.int32

NP = 50
NQ = 25
OW = 4
NO = 64
PAIRS = ((0, 1), (0, 2), (0, 3), (1, 2), (1, 3), (2, 3))
SLOT = 64
ZN = 8
YH = 2


def iota(shape, dim):
    return lax.broadcasted_iota(I32, shape, dim)


def dot(a, b, dims):
    return lax.dot_general(a, b, (dims, ((), ())), preferred_element_type=F32)


class Plan:
    def __init__(self, lanes, cap, slots):
        self.lanes, self.cap, self.slots = lanes, cap, slots
        self.msg = slots * SLOT
        self.group = 128 // cap
        self.full = NQ // self.group
        self.wide = self.group * lanes // 128
        self.last = -(-lanes // 128)
        self.span = self.full * self.wide + self.last
        self.rest = -(-2 * (self.full + 1) // 16)
        self.count = 3 * self.span + self.rest * self.wide
        self.depth = (self.full + 1) * 128


NN = ((1,), (0,))
NT = ((1,), (1,))
TN = ((0,), (0,))


def kernel(plan, amps, integral, occ_row, occ, virt, out, blk, wblk, rest32, st, sw, ex, y32, texp, wall, c32, keep, psend,
           precv, msg, p2r, zmat, tile, p3r, ag_s, ag_r, w_s, w_r, d_s, d_r, p2_s, p2_rs, p3_s, p3_rs, word):
    group, wide, span, full = plan.group, plan.wide, plan.span, plan.full
    dense = plan.lanes == OW * NO
    row = lax.axis_index("row")
    col = lax.axis_index("col")
    core = row % 2
    chip = row // 2
    yh = col // ZN
    z = col % ZN

    right = yh * ZN + (z + 1) % ZN
    left = yh * ZN + (z + ZN - 1) % ZN
    opposite = (1 - yh) * ZN + z
    mate = row + 1 - 2 * core
    home = chip // ZN
    home_z = chip % ZN
    late_owner = home_z == (z + 4) % ZN
    mirror_col = row // 2
    own_p2 = (home == yh).astype(I32)
    own_p3 = (mirror_col == col).astype(I32)

    x, y = row // 8, yh * 4 + chip % 4

    def at_x(d):
        return ((x + 4 + d) % 4 * 8 + row % 8, col)

    def at_y(d):
        to = (y + 8 + d) % 8
        return (x * 8 + to % 4 * 2 + core, to // 4 * ZN + z)

    def at_z(d):
        return (row, yh * ZN + (z + ZN + d) % ZN)

    bar = pltpu.get_barrier_semaphore()
    near = [at(d) for at in (at_x, at_y, at_z) for d in (1, -1)] + [(mate, col)]
    for to in near:
        pl.semaphore_signal(bar, inc=1, device_id=to, device_id_type=MESH)

    rounds = (
        ((at_y, 1), (at_y, -1)), ((at_x, 1), (at_x, -1), (at_y, 2), (at_y, -2)), ((at_y, 3), (at_y, -3)),
        (None,), ((at_z, 1), (at_z, -1)), ((at_z, 2), (at_z, -2)), ((at_z, 1),))

    def tell(n):
        for way, to in enumerate(rounds[n]):
            pl.semaphore_signal(word.at[4 * n + way], inc=1, device_id=(mate, col) if to is None else to[0](to[1]),
                                device_id_type=MESH)

    def hear(n):
        for way in range(len(rounds[n])):
            pl.semaphore_wait(word.at[4 * n + way], 1)

    block_irrep = virt[row // 4]
    lab = occ_row[...]

    def offsets(label):
        counts = [jnp.sum(jnp.where(lab == (label ^ occ[i]), 1.0, 0.0), axis=1, keepdims=True).astype(I32) for i in range(OW)]
        if dense:
            return [jnp.full((1, 1), i * NO, I32) for i in range(OW)], [jnp.full((1, 1), NO, I32)] * OW
        return [sum(counts[:i], jnp.zeros((1, 1), I32)) for i in range(OW)], counts

    def by_window(which, values):
        return jnp.where(which == 0, values[0], jnp.where(which == 1, values[1], jnp.where(which == 2, values[2], values[3])))

    labf = lab.astype(F32)
    r256, l64 = iota((256, NO), 0), iota((256, NO), 1)
    here = virt[col // 2] ^ block_irrep
    here_off, _ = offsets(here)
    pl_lane = iota((1, group * plan.lanes), 1)

    def select(ref, k_of, i_of):
        hk = jnp.sum(jnp.where(l64 == k_of, labf, 0.0), axis=1, keepdims=True)
        k1, i1 = k_of[:, :1], i_of[:, :1]
        hi = by_window(i1, [occ[i] for i in range(OW)])
        if dense:
            place = k1
        else:
            same = (labf == hk) & (l64 < k_of)
            place = jnp.sum(jnp.where(same, 1.0, 0.0), axis=1, keepdims=True).astype(I32)
        key = jnp.where((hk.astype(I32) ^ hi) == here, by_window(i1, here_off) + place, -1)
        for g in range(group):
            hit = (key == pl_lane % plan.lanes) & (pl_lane // plan.lanes == g)
            ref[g * 256:(g + 1) * 256, :] = jnp.where(hit, 1.0, 0.0).astype(BF16)

    def pack(planes, sel, dst):
        for q in range(full + 1):
            cs = range(q * group, min(NQ, (q + 1) * group))
            many = wide if q < full else plan.last
            x = jnp.concatenate([planes[c] for c in cs], axis=1)
            y = dot(x, sel[0:len(cs) * 256, 0:many * 128], NN)
            for r in range(3):
                for t in range(many):
                    dst[r * span + q * wide + t] = y[r * 16:(r + 1) * 16, t * 128:(t + 1) * 128].astype(BF16)
            rest32[2 * q:2 * q + 2, 0:many * 128] = y[48:50, :]
        for r in range(plan.rest):
            for t in range(wide):
                dst[3 * span + r * wide + t] = rest32[r * 16:(r + 1) * 16, t * 128:(t + 1) * 128].astype(BF16)

    def expand(src, sel, dst):
        lines = [jnp.concatenate([src[r * span + q * wide + t] for t in range(wide)], axis=1)
                 for q in range(full) for r in range(3)]
        lines += [jnp.concatenate([src[3 * span + r * wide + t] for t in range(wide)], axis=1) for r in range(plan.rest)]
        tall = 48 * full
        y32[0:tall + 16 * plan.rest, :] = dot(jnp.concatenate(lines, axis=0), sel[...], NN)
        x = jnp.concatenate([jnp.concatenate([src[r * span + full * wide + t] for t in range(plan.last)], axis=1)
                             for r in range(3)], axis=0)
        z6 = dot(x, sel[0:plan.last * 128, :], NN)
        for q in range(full + 1):
            for i in range(OW):
                lanes = slice(i * 128, (i + 1) * 128)
                main = y32[q * 48:(q + 1) * 48, lanes] if q < full else z6[:, lanes]
                dst[i * SLOT:i * SLOT + 48, q * 128:(q + 1) * 128] = main.astype(BF16)
                dst[i * SLOT + 48:i * SLOT + 50, q * 128:(q + 1) * 128] = (
                    y32[tall + 2 * q:tall + 2 * q + 2, lanes].astype(BF16))

    rest32[...] = jnp.zeros(rest32.shape, F32)
    select(st, r256 % NO, r256 // NO)
    pack(amps, st, blk.at[z])

    pl.semaphore_wait(bar, len(near))

    cut = plan.count // 2
    parts = ((0, cut), (cut, plan.count - cut))

    def moved(direction, step, part, src):
        lo, size = parts[part]
        n = (direction * 4 + step) * 2 + part
        ref = blk.at[src, pl.ds(lo, size)]
        return pltpu.make_async_remote_copy(
            src_ref=ref, dst_ref=ref, send_sem=ag_s.at[n], recv_sem=ag_r.at[n],
            device_id=(row, right if direction == 0 else left), device_id_type=MESH)

    def hop(direction, step, part):
        return moved(direction, step, part, (z + ZN - step) % ZN if direction == 0 else (z + step) % ZN)

    def arrival(direction, step, part):
        return moved(direction, step, part, (z + ZN - step - 1) % ZN if direction == 0 else (z + step + 1) % ZN)

    for part in range(2):
        for d in range(2):
            hop(d, 0, part).start()

    tell(0)
    select(sw, r256 // OW, r256 % OW)
    pack(integral, sw, wblk.at[yh])
    hear(0)
    tell(1)

    def swap(which):
        return pltpu.make_async_remote_copy(
            src_ref=wblk.at[which], dst_ref=wblk.at[which], send_sem=w_s, recv_sem=w_r, device_id=(row, opposite),
            device_id_type=MESH)

    er = iota((group * plan.lanes, 1), 0)
    el = iota((1, 512), 1)
    e_i, e_g, e_m = el // 128, (el % 128) // plan.cap, el % plan.cap
    for n in range(5):
        label = block_irrep ^ (virt[yh * 4 + n] if n < 4 else virt[(1 - yh) * 4 + z // 2])
        off, counts = offsets(label)
        key = jnp.where(e_m < by_window(e_i, counts), by_window(e_i, off) + e_m, -1)
        hit = (er % plan.lanes == key) & (er // plan.lanes == e_g)
        ex[n] = jnp.where(hit, 1.0, 0.0).astype(BF16)

    def slots(label):
        alive = [(occ[i] ^ occ[j]) == label for i, j in PAIRS]
        if plan.slots == len(PAIRS):
            return [[alive[p] if p == n else None for p in range(len(PAIRS))] for n in range(plan.slots)]
        ones = [jnp.where(a, 1, 0) for a in alive]
        return [[alive[p] & (sum(ones[:p], 0) == n) if p >= n else None for p in range(len(PAIRS))]
                for n in range(plan.slots)]

    def spread_matrix():
        zr, zl = iota((plan.msg, OW * 256), 0), iota((plan.msg, OW * 256), 1)
        zr1 = zr[:, :1]
        first = second = jnp.full((plan.msg, 1), -1, I32)
        for n, taken in enumerate(slots(here)):
            for p, (i, j) in enumerate(PAIRS):
                if taken[p] is not None:
                    it = (zr1 // SLOT == n) & taken[p]
                    first, second = jnp.where(it, i, first), jnp.where(it, j, second)
        zb = zr1 % SLOT
        zl1 = zl[:1]
        zi, zt = zl1 // 256, zl1 % 256
        in_b = (zt // OW == zb) & (zb < NP)
        plus = in_b & (zi == first) & (zt % OW == second)
        minus = in_b & (zi == second) & (zt % OW == first)
        zmat[...] = (jnp.where(plus, 1.0, 0.0) - jnp.where(minus, 1.0, 0.0)).astype(BF16)

    low = iota((32, 128), 1) < SLOT
    order = (0, ZN - 1, 1, ZN - 2, 2, ZN - 3, 3, 4)

    def unpack(n):
        za = (z + order[n]) % ZN
        expand(blk.at[za], ex.at[za // 2], texp.at[n])

    def mate_copy(n):
        return pltpu.make_async_remote_copy(
            src_ref=psend.at[n], dst_ref=precv.at[n], send_sem=d_s.at[n], recv_sem=d_r.at[n], device_id=(mate, col),
            device_id_type=MESH)

    def differences(n):
        za = (z + order[n]) % ZN
        for h in range(YH):
            c32[:, h * 256:(h + 1) * 256] = dot(texp[n], wall[h], NT)
        la = virt[(yh * ZN + za) // 2]
        taken_by = [slots(la ^ virt[(h * ZN + z) // 2]) for h in range(YH)]
        halves = []
        for half in range(2):
            line = []
            for h in range(YH):
                values = []
                for i, j in PAIRS:

                    def piece(r, q):
                        start = SLOT * r + NQ * half
                        v = c32[start:start + 32, h * 256 + (q // 2) * 128:h * 256 + (q // 2) * 128 + 128]
                        return v if q % 2 == 0 else pltpu.roll(v, SLOT, axis=1)

                    values.append(piece(i, j) - piece(j, i))
                pieces = []
                for n, taken in enumerate(taken_by[h]):
                    v = sum(values[p] * jnp.where(t, 1.0, 0.0) for p, t in enumerate(taken) if t is not None)
                    pieces.append(v if n % 2 == 0 else pltpu.roll(v, SLOT, axis=1))
                for n in range(0, plan.slots, 2):
                    line.append(jnp.where(low, pieces[n], pieces[n + 1]))
            halves.append(jnp.concatenate(line, axis=1))
        return halves

    def compute(n):
        halves = differences(n)
        keep[n] = jnp.where(core == 0, halves[0], halves[1])
        psend[n] = jnp.where(core == 0, halves[1], halves[0]).astype(BF16)
        mate_copy(n).start()

    def deliver(m, to_row, h, place):
        mine = (to_row == row) & (yh == h)

        @pl.when(jnp.logical_not(mine))
        def _():
            pltpu.make_async_remote_copy(
                src_ref=msg.at[m], dst_ref=p2r.at[place], send_sem=p2_s, recv_sem=p2_rs,
                device_id=(to_row, h * ZN + z), device_id_type=MESH).start()

        @pl.when(mine)
        def _():
            pltpu.make_async_copy(msg.at[m], p2r.at[place], p2_rs).start()

    def finish(n):
        za = (z + order[n]) % ZN
        mate_copy(n).wait_recv()
        total = (keep[n] + precv[n].astype(F32)).astype(BF16)
        for h in range(YH):
            msg[2 * n + h] = total[:, h * plan.msg:(h + 1) * plan.msg]
            deliver(2 * n + h, 2 * (yh * ZN + za) + core, h, chip)

    def forward(step):
        for part in range(2):
            for d in range(2):
                arrival(d, step - 1, part).wait_recv()
                if step < 3 or part == d:
                    hop(d, step, part).start()

    hear(1)
    swap(yh).start()
    tell(2)
    forward(1)
    texp[...] = jnp.zeros(texp.shape, BF16)
    wall[...] = jnp.zeros(wall.shape, BF16)
    expand(wblk.at[yh], ex.at[z // 2], wall.at[yh])
    unpack(0)
    hear(2)
    tell(3)
    unpack(1)
    unpack(2)
    forward(2)
    hear(3)
    tell(4)
    spread_matrix()
    unpack(3)
    unpack(4)
    swap(1 - yh).wait_recv()
    expand(wblk.at[1 - yh], ex.at[4], wall.at[1 - yh])
    compute(0)
    compute(1)
    forward(3)
    hear(4)
    tell(5)
    for n in range(2, 7):
        if n > 4:
            unpack(n)
        compute(n)
        finish(n - 2)
    hear(5)
    tell(6)
    finish(5)
    finish(6)
    for d in range(2):
        arrival(d, 3, d).wait_recv()
    unpack(7)
    halves = differences(7)
    za = (z + order[7]) % ZN
    for half in range(2):
        total = halves[half].astype(BF16)
        for h in range(YH):
            m = 14 + 2 * half + h
            msg[m] = total[:, h * plan.msg:(h + 1) * plan.msg]
            deliver(m, 2 * (yh * ZN + za) + half, h, row)

    def add_up(many):
        pltpu.make_async_copy(p2r.at[pl.ds(0, many)], p2r.at[pl.ds(0, many)], p2_rs).wait()
        total = p2r[0].astype(F32)
        for n in range(1, many):
            total = total + p2r[n].astype(F32)
        tile[...] = total.astype(BF16)

    @pl.when(late_owner)
    def _():
        add_up(32)

    @pl.when(jnp.logical_not(late_owner))
    def _():
        add_up(16)

    hear(6)
    def mirror_copy(s):
        return pltpu.make_async_remote_copy(
            src_ref=tile, dst_ref=p3r.at[row % 2], send_sem=p3_s.at[s], recv_sem=p3_rs.at[row % 2],
            device_id=(2 * col + s, mirror_col), device_id_type=MESH)

    for s in range(2):
        self_mirror = (2 * col + s == row) & (mirror_col == col)

        @pl.when(jnp.logical_not(self_mirror))
        def _():
            mirror_copy(s).start()

        @pl.when(self_mirror)
        def _():
            pltpu.make_async_copy(tile, p3r.at[s], p3_rs.at[s]).start()

    base = dot(tile[...], zmat[...], NN)
    br, bl = iota((32, 256), 0), iota((32, 256), 1)
    spread = None
    for s in range(2):
        pltpu.make_async_copy(p3r.at[s], p3r.at[s], p3_rs.at[s]).wait()
        put = ((bl % 128) == br + NQ * s + SLOT * (bl // 128)) & (br < NQ)
        part = dot(p3r[s], jnp.where(put, 1.0, 0.0).astype(BF16), TN)
        spread = part if spread is None else spread + part
    line = []
    for t in range(plan.slots // 2):
        both = []
        for u in range(2):
            lo = (2 * t + u) * SLOT
            a0 = spread[lo:lo + 32, u * 128:(u + 1) * 128]
            a1 = spread[lo + NQ:lo + NQ + 32, u * 128:(u + 1) * 128]
            both.append(jnp.where(row % 2 == 0, a0, a1))
        line.append(both[0] + both[1])
    swapped = jnp.concatenate(line, axis=1).astype(BF16)
    res = base - dot(swapped, zmat[...], NN)
    for i in range(OW):
        out[i] = res[0:NQ, i * 256:i * 256 + NP * OW]

    for part in range(2):
        for d in range(2):
            for step in range(4):
                if step < 3 or part == d:
                    hop(d, step, part).wait_send()
    swap(yh).wait_send()
    for n in range(7):
        mate_copy(n).wait_send()

    @pl.when(home == yh)
    def _():
        pltpu.make_async_copy(msg.at[pl.ds(0, 17)], msg.at[pl.ds(0, 17)], p2_s).wait()

    @pl.when(home != yh)
    def _():
        pltpu.make_async_copy(msg, msg, p2_s).wait()

    for s in range(2):
        @pl.when(jnp.logical_not((2 * col + s == row) & (mirror_col == col)))
        def _():
            mirror_copy(s).wait_send()


def call(lanes, cap, slots, collective_id, amps, integral, virt_irrep, occ_irrep):
    plan = Plan(lanes, cap, slots)
    vmem = pl.BlockSpec(memory_space=pltpu.VMEM)
    smem = pl.BlockSpec(memory_space=pltpu.SMEM)
    dma = pltpu.SemaphoreType.DMA
    return pl.pallas_call(
        functools.partial(kernel, plan),
        out_shape=jax.ShapeDtypeStruct((OW, NQ, NP * OW), F32),
        in_specs=[vmem, vmem, vmem, smem, smem],
        out_specs=vmem,
        scratch_shapes=[
            pltpu.VMEM((ZN, plan.count, 16, 128), BF16),
            pltpu.VMEM((YH, plan.count, 16, 128), BF16),
            pltpu.VMEM((plan.rest * 16, plan.wide * 128), F32),
            pltpu.VMEM((plan.group * 256, plan.wide * 128), BF16),
            pltpu.VMEM((plan.group * 256, plan.wide * 128), BF16),
            pltpu.VMEM((5, plan.wide * 128, 512), BF16),
            pltpu.VMEM((48 * plan.full + 16 * plan.rest, 512), F32),
            pltpu.VMEM((ZN, OW * SLOT, plan.depth), BF16),
            pltpu.VMEM((YH, OW * SLOT, plan.depth), BF16),
            pltpu.VMEM((OW * SLOT, 512), F32),
            pltpu.VMEM((ZN - 1, 32, YH * plan.msg), F32),
            pltpu.VMEM((ZN - 1, 32, YH * plan.msg), BF16),
            pltpu.VMEM((ZN - 1, 32, YH * plan.msg), BF16),
            pltpu.VMEM((18, 32, plan.msg), BF16),
            pltpu.VMEM((32, 32, plan.msg), BF16),
            pltpu.VMEM((plan.msg, OW * 256), BF16),
            pltpu.VMEM((32, plan.msg), BF16),
            pltpu.VMEM((2, 32, plan.msg), BF16),
            dma((16,)), dma((16,)), dma, dma, dma((ZN - 1,)), dma((ZN - 1,)), dma, dma, dma((2,)), dma((2,)),
            pltpu.SemaphoreType.REGULAR((28,)),
        ],
        name="cycle%d" % lanes,
        compiler_params=pltpu.CompilerParams(
            collective_id=collective_id, has_side_effects=True, vmem_limit_bytes=48 * 2**20),
    )(amps, integral, occ_irrep.reshape(1, NO), occ_irrep, virt_irrep)


TIERS = ((64, 32, 2), (96, 32, 4), (OW * NO, NO, 6))


def shards(amps, integral, virt_irrep, occ_irrep):
    partner = jnp.concatenate([occ_irrep[:OW], jnp.zeros((1,), I32)])
    weight = np.full((NO, OW + 1, 1), 1, np.int32)
    weight[:, OW] = 1 << 10
    weight[:OW, :OW] += 1 << 18
    irreps = jnp.arange(8, dtype=I32)
    hits = (occ_irrep[:, None, None] ^ partner[None, :, None]) == irreps
    sums = jnp.sum(jnp.where(hits, weight, 0), axis=(0, 1))
    need = sums % (1 << 10)
    most = (sums % (1 << 18)) // (1 << 10)
    pairs = (sums // (1 << 18) - jnp.where(irreps == 0, OW, 0)) // 2
    tier = jnp.zeros((8,), I32)
    for lanes, cap, slots in TIERS[:-1]:
        tier = tier + jnp.where((need > lanes) | (most > cap) | (pairs > slots), 1, 0)
    tier = jnp.max(tier)
    calls = [functools.partial(call, lanes, cap, slots, n) for n, (lanes, cap, slots) in enumerate(TIERS)]
    tile = lax.switch(tier, calls, amps.transpose(1, 0, 2), integral, virt_irrep, occ_irrep)
    return tile.transpose(1, 0, 2)


def solution(mesh):
    placed = (P("col", "row", None), P("row", "col", None), P(), P())
    return jax.shard_map(
        shards, mesh=mesh, in_specs=placed, out_specs=P("row", None, "col"), check_vma=False
    )
```

```python
import functools

import jax
import jax.numpy as jnp
import numpy as np
from jax import lax
from jax.experimental import pallas as pl
from jax.experimental.pallas import tpu as pltpu
from jax.sharding import PartitionSpec as P

MESH = pl.DeviceIdType.MESH
F32 = jnp.float32
BF16 = jnp.bfloat16
I32 = jnp.int32

NP = 50
NQ = 25
OW = 4
NO = 64
PAIRS = ((0, 1), (0, 2), (0, 3), (1, 2), (1, 3), (2, 3))
SLOT = 64
ZN = 8
YH = 2


def iota(shape, dim):
    return lax.broadcasted_iota(I32, shape, dim)


def dot(a, b, dims):
    return lax.dot_general(a, b, (dims, ((), ())), preferred_element_type=F32)


class Plan:
    def __init__(self, lanes, cap, slots):
        self.lanes, self.cap, self.slots = lanes, cap, slots
        self.msg = slots * SLOT
        self.parts = 2
        self.near = 2 if slots == 2 else 3
        self.paired = 2 * self.near - 1
        self.messages = 2 * self.paired + 4 * (ZN - self.paired)
        self.direct = slots == 2
        self.group = 128 // cap
        self.full = NQ // self.group
        self.wide = self.group * lanes // 128
        self.last = -(-lanes // 128)
        self.span = self.full * self.wide + self.last
        self.rest = -(-2 * (self.full + 1) // 16)
        self.count = 3 * self.span + self.rest * self.wide
        self.depth = (self.full + 1) * 128


NN = ((1,), (0,))
NT = ((1,), (1,))
TN = ((0,), (0,))


def kernel(plan, amps, integral, occ_row, occ, virt, out, blk, wblk, rest32, st, sw, ex, y32, texp, wall, c32, keep, psend,
           precv, msg, p2r, zmat, tile, p3r, ag_s, ag_r, w_s, w_r, d_s, d_r, p2_s, p2_rs, p3_s, p3_rs, mir, m_s, m_rs, word):
    group, wide, span, full = plan.group, plan.wide, plan.span, plan.full
    dense = plan.lanes == OW * NO
    row = lax.axis_index("row")
    col = lax.axis_index("col")
    core = row % 2
    chip = row // 2
    yh = col // ZN
    z = col % ZN

    right = yh * ZN + (z + 1) % ZN
    left = yh * ZN + (z + ZN - 1) % ZN
    opposite = (1 - yh) * ZN + z
    mate = row + 1 - 2 * core
    home = chip // ZN
    home_z = chip % ZN
    gap = (home_z + ZN - z) % ZN
    late_owner = (gap >= plan.near) & (gap <= ZN - plan.near)
    mirror_col = row // 2

    x, y = row // 8, yh * 4 + chip % 4

    def at_x(d):
        return ((x + 4 + d) % 4 * 8 + row % 8, col)

    def at_y(d):
        to = (y + 8 + d) % 8
        return (x * 8 + to % 4 * 2 + core, to // 4 * ZN + z)

    def at_z(d):
        return (row, yh * ZN + (z + ZN + d) % ZN)

    bar = pltpu.get_barrier_semaphore()
    near = [at(d) for at in (at_x, at_y, at_z) for d in (1, -1)] + [(mate, col)]
    for to in near:
        pl.semaphore_signal(bar, inc=1, device_id=to, device_id_type=MESH)

    rounds = (
        ((at_y, 1), (at_y, -1)), ((at_x, 1), (at_x, -1), (at_y, 2), (at_y, -2)), ((at_y, 3), (at_y, -3)),
        (None,), ((at_z, 1), (at_z, -1)), ((at_z, 2), (at_z, -2)), ((at_z, 1),))

    def tell(n):
        for way, to in enumerate(rounds[n]):
            pl.semaphore_signal(word.at[4 * n + way], inc=1, device_id=(mate, col) if to is None else to[0](to[1]),
                                device_id_type=MESH)

    def hear(n):
        for way in range(len(rounds[n])):
            pl.semaphore_wait(word.at[4 * n + way], 1)

    block_irrep = virt[row // 4]
    lab = occ_row[...]

    def offsets(label):
        counts = [jnp.sum(jnp.where(lab == (label ^ occ[i]), 1.0, 0.0), axis=1, keepdims=True).astype(I32) for i in range(OW)]
        if dense:
            return [jnp.full((1, 1), i * NO, I32) for i in range(OW)], [jnp.full((1, 1), NO, I32)] * OW
        return [sum(counts[:i], jnp.zeros((1, 1), I32)) for i in range(OW)], counts

    def by_window(which, values):
        return jnp.where(which == 0, values[0], jnp.where(which == 1, values[1], jnp.where(which == 2, values[2], values[3])))

    labf = lab.astype(F32)
    r256, l64 = iota((256, NO), 0), iota((256, NO), 1)
    here = virt[col // 2] ^ block_irrep
    here_off, _ = offsets(here)
    pl_lane = iota((1, group * plan.lanes), 1)

    def select(ref, k_of, i_of):
        hk = jnp.sum(jnp.where(l64 == k_of, labf, 0.0), axis=1, keepdims=True)
        k1, i1 = k_of[:, :1], i_of[:, :1]
        hi = by_window(i1, [occ[i] for i in range(OW)])
        if dense:
            place = k1
        else:
            same = (labf == hk) & (l64 < k_of)
            place = jnp.sum(jnp.where(same, 1.0, 0.0), axis=1, keepdims=True).astype(I32)
        key = jnp.where((hk.astype(I32) ^ hi) == here, by_window(i1, here_off) + place, -1)
        for g in range(group):
            hit = (key == pl_lane % plan.lanes) & (pl_lane // plan.lanes == g)
            ref[g * 256:(g + 1) * 256, :] = jnp.where(hit, 1.0, 0.0).astype(BF16)

    def pack(planes, sel, dst):
        for q in range(full + 1):
            cs = range(q * group, min(NQ, (q + 1) * group))
            many = wide if q < full else plan.last
            x = jnp.concatenate([planes[c] for c in cs], axis=1)
            y = dot(x, sel[0:len(cs) * 256, 0:many * 128], NN)
            for r in range(3):
                for t in range(many):
                    dst[r * span + q * wide + t] = y[r * 16:(r + 1) * 16, t * 128:(t + 1) * 128].astype(BF16)
            rest32[2 * q:2 * q + 2, 0:many * 128] = y[48:50, :]
        for r in range(plan.rest):
            for t in range(wide):
                dst[3 * span + r * wide + t] = rest32[r * 16:(r + 1) * 16, t * 128:(t + 1) * 128].astype(BF16)

    def expand(src, sel, dst):
        lines = [jnp.concatenate([src[r * span + q * wide + t] for t in range(wide)], axis=1)
                 for q in range(full) for r in range(3)]
        lines += [jnp.concatenate([src[3 * span + r * wide + t] for t in range(wide)], axis=1) for r in range(plan.rest)]
        tall = 48 * full
        y32[0:tall + 16 * plan.rest, :] = dot(jnp.concatenate(lines, axis=0), sel[...], NN)
        x = jnp.concatenate([jnp.concatenate([src[r * span + full * wide + t] for t in range(plan.last)], axis=1)
                             for r in range(3)], axis=0)
        z6 = dot(x, sel[0:plan.last * 128, :], NN)
        for q in range(full + 1):
            for i in range(OW):
                lanes = slice(i * 128, (i + 1) * 128)
                main = y32[q * 48:(q + 1) * 48, lanes] if q < full else z6[:, lanes]
                dst[i * SLOT:i * SLOT + 48, q * 128:(q + 1) * 128] = main.astype(BF16)
                dst[i * SLOT + 48:i * SLOT + 50, q * 128:(q + 1) * 128] = (
                    y32[tall + 2 * q:tall + 2 * q + 2, lanes].astype(BF16))

    rest32[...] = jnp.zeros(rest32.shape, F32)
    select(st, r256 % NO, r256 // NO)
    pack(amps, st, blk.at[z])

    pl.semaphore_wait(bar, len(near))

    edges = [plan.count * n // plan.parts for n in range(plan.parts + 1)]

    def goes(direction, step, part):
        return step < 3 or (part < plan.parts // 2) == (direction == 0)

    def moved(direction, step, part, src):
        n = (direction * 4 + step) * plan.parts + part
        ref = blk.at[src, pl.ds(edges[part], edges[part + 1] - edges[part])]
        return pltpu.make_async_remote_copy(
            src_ref=ref, dst_ref=ref, send_sem=ag_s.at[n], recv_sem=ag_r.at[n],
            device_id=(row, right if direction == 0 else left), device_id_type=MESH)

    def hop(direction, step, part):
        return moved(direction, step, part, (z + ZN - step) % ZN if direction == 0 else (z + step) % ZN)

    def arrival(direction, step, part):
        return moved(direction, step, part, (z + ZN - step - 1) % ZN if direction == 0 else (z + step + 1) % ZN)

    for part in range(plan.parts):
        for d in range(2):
            hop(d, 0, part).start()

    tell(0)
    select(sw, r256 // OW, r256 % OW)
    pack(integral, sw, wblk.at[yh])
    hear(0)
    tell(1)

    def swap(which):
        return pltpu.make_async_remote_copy(
            src_ref=wblk.at[which], dst_ref=wblk.at[which], send_sem=w_s, recv_sem=w_r, device_id=(row, opposite),
            device_id_type=MESH)

    er = iota((group * plan.lanes, 1), 0)
    el = iota((1, 512), 1)
    e_i, e_g, e_m = el // 128, (el % 128) // plan.cap, el % plan.cap
    for n in range(5):
        label = block_irrep ^ (virt[yh * 4 + n] if n < 4 else virt[(1 - yh) * 4 + z // 2])
        off, counts = offsets(label)
        key = jnp.where(e_m < by_window(e_i, counts), by_window(e_i, off) + e_m, -1)
        hit = (er % plan.lanes == key) & (er // plan.lanes == e_g)
        ex[n] = jnp.where(hit, 1.0, 0.0).astype(BF16)

    def slots(label):
        alive = [(occ[i] ^ occ[j]) == label for i, j in PAIRS]
        if plan.slots == len(PAIRS):
            return [[alive[p] if p == n else None for p in range(len(PAIRS))] for n in range(plan.slots)]
        ones = [jnp.where(a, 1, 0) for a in alive]
        return [[alive[p] & (sum(ones[:p], 0) == n) if p >= n else None for p in range(len(PAIRS))]
                for n in range(plan.slots)]

    def spread_matrix():
        zr, zl = iota((plan.msg, OW * 256), 0), iota((plan.msg, OW * 256), 1)
        zr1 = zr[:, :1]
        first = second = jnp.full((plan.msg, 1), -1, I32)
        for n, taken in enumerate(slots(here)):
            for p, (i, j) in enumerate(PAIRS):
                if taken[p] is not None:
                    it = (zr1 // SLOT == n) & taken[p]
                    first, second = jnp.where(it, i, first), jnp.where(it, j, second)
        zb = zr1 % SLOT
        zl1 = zl[:1]
        zi, zt = zl1 // 256, zl1 % 256
        in_b = (zt // OW == zb) & (zb < NP)
        plus = in_b & (zi == first) & (zt % OW == second)
        minus = in_b & (zi == second) & (zt % OW == first)
        zmat[...] = (jnp.where(plus, 1.0, 0.0) - jnp.where(minus, 1.0, 0.0)).astype(BF16)

    low = iota((32, 128), 1) < SLOT
    order = (0, ZN - 1, 1, ZN - 2, 2, ZN - 3, 3, 4)

    def unpack(n):
        za = (z + order[n]) % ZN
        expand(blk.at[za], ex.at[za // 2], texp.at[n])

    def mate_copy(n):
        return pltpu.make_async_remote_copy(
            src_ref=psend.at[n], dst_ref=precv.at[n], send_sem=d_s.at[n], recv_sem=d_r.at[n], device_id=(mate, col),
            device_id_type=MESH)

    def differences(n):
        za = (z + order[n]) % ZN
        for h in range(YH):
            c32[:, h * 256:(h + 1) * 256] = dot(texp[n], wall[h], NT)
        la = virt[(yh * ZN + za) // 2]
        taken_by = [slots(la ^ virt[(h * ZN + z) // 2]) for h in range(YH)]
        halves = []
        for half in range(2):
            line = []
            for h in range(YH):
                values = []
                for i, j in PAIRS:

                    def piece(r, q):
                        start = SLOT * r + NQ * half
                        v = c32[start:start + 32, h * 256 + (q // 2) * 128:h * 256 + (q // 2) * 128 + 128]
                        return v if q % 2 == 0 else pltpu.roll(v, SLOT, axis=1)

                    values.append(piece(i, j) - piece(j, i))
                pieces = []
                for n, taken in enumerate(taken_by[h]):
                    v = sum(values[p] * jnp.where(t, 1.0, 0.0) for p, t in enumerate(taken) if t is not None)
                    pieces.append(v if n % 2 == 0 else pltpu.roll(v, SLOT, axis=1))
                for n in range(0, plan.slots, 2):
                    line.append(jnp.where(low, pieces[n], pieces[n + 1]))
            halves.append(jnp.concatenate(line, axis=1))
        return halves

    def compute(n):
        halves = differences(n)
        keep[n] = jnp.where(core == 0, halves[0], halves[1])
        psend[n] = jnp.where(core == 0, halves[1], halves[0]).astype(BF16)
        mate_copy(n).start()

    def deliver(m, to_row, h, place):
        mine = (to_row == row) & (yh == h)

        @pl.when(jnp.logical_not(mine))
        def _():
            pltpu.make_async_remote_copy(
                src_ref=msg.at[m], dst_ref=p2r.at[place], send_sem=p2_s, recv_sem=p2_rs,
                device_id=(to_row, h * ZN + z), device_id_type=MESH).start()

        @pl.when(mine)
        def _():
            pltpu.make_async_copy(msg.at[m], p2r.at[place], p2_rs).start()

    def finish(n):
        za = (z + order[n]) % ZN
        mate_copy(n).wait_recv()
        total = (keep[n] + precv[n].astype(F32)).astype(BF16)
        for h in range(YH):
            msg[2 * n + h] = total[:, h * plan.msg:(h + 1) * plan.msg]
            deliver(2 * n + h, 2 * (yh * ZN + za) + core, h, chip)

    def spread_out(n):
        halves = differences(n)
        za = (z + order[n]) % ZN
        first = 2 * plan.paired + 4 * (n - plan.paired)
        for h in range(YH):
            m = first + 2 * h
            for half in range(2):
                msg[m + half] = halves[half][:, h * plan.msg:(h + 1) * plan.msg].astype(BF16)
            if plan.direct and n == 7:
                for half in range(2):
                    pltpu.make_async_remote_copy(
                        src_ref=msg.at[pl.ds(m, 2)], dst_ref=mir.at[row], send_sem=m_s, recv_sem=m_rs,
                        device_id=(2 * (h * ZN + z) + half, yh * ZN + za), device_id_type=MESH).start()
            for half in range(2):
                deliver(m + half, 2 * (yh * ZN + za) + half, h, row)

    def work(n):
        if n < plan.paired:
            compute(n)
        else:
            spread_out(n)

    def forward(step):
        for part in range(plan.parts):
            for d in range(2):
                arrival(d, step - 1, part).wait_recv()
                if goes(d, step, part):
                    hop(d, step, part).start()

    hear(1)
    swap(yh).start()
    tell(2)
    forward(1)
    texp[...] = jnp.zeros(texp.shape, BF16)
    wall[...] = jnp.zeros(wall.shape, BF16)
    expand(wblk.at[yh], ex.at[z // 2], wall.at[yh])
    unpack(0)
    hear(2)
    tell(3)
    unpack(1)
    unpack(2)
    forward(2)
    hear(3)
    tell(4)
    spread_matrix()
    unpack(3)
    unpack(4)
    swap(1 - yh).wait_recv()
    expand(wblk.at[1 - yh], ex.at[4], wall.at[1 - yh])
    for n in range(2):
        work(n)
    forward(3)
    hear(4)
    tell(5)
    waiting = list(range(plan.paired))
    for n in range(2, 7):
        if n > 4:
            unpack(n)
        work(n)
        if waiting:
            finish(waiting.pop(0))
    for n in waiting:
        finish(n)
    hear(5)
    tell(6)
    hear(6)
    for part in range(plan.parts):
        for d in range(2):
            if goes(d, 3, part):
                arrival(d, 3, part).wait_recv()
    unpack(7)
    work(7)

    def add_up(many):
        pltpu.make_async_copy(p2r.at[pl.ds(0, many)], p2r.at[pl.ds(0, many)], p2_rs).wait()
        total = p2r[0].astype(F32)
        for n in range(1, many):
            total = total + p2r[n].astype(F32)
        tile[...] = total.astype(BF16)

    @pl.when(late_owner)
    def _():
        add_up(32)

    @pl.when(jnp.logical_not(late_owner))
    def _():
        add_up(16)

    def mirror_copy(s):
        return pltpu.make_async_remote_copy(
            src_ref=tile, dst_ref=p3r.at[row % 2], send_sem=p3_s.at[s], recv_sem=p3_rs.at[row % 2],
            device_id=(2 * col + s, mirror_col), device_id_type=MESH)

    late_mirror = (gap == 4) if plan.direct else (gap < 0)

    @pl.when(jnp.logical_not(late_mirror))
    def _():
        for s in range(2):
            self_mirror = (2 * col + s == row) & (mirror_col == col)

            @pl.when(jnp.logical_not(self_mirror))
            def _():
                mirror_copy(s).start()

            @pl.when(self_mirror)
            def _():
                pltpu.make_async_copy(tile, p3r.at[s], p3_rs.at[s]).start()

    base = dot(tile[...], zmat[...], NN)

    if plan.direct:
        @pl.when(late_mirror)
        def _():
            pltpu.make_async_copy(mir, mir, m_rs).wait()
            for s in range(2):
                total = mir[0, s].astype(F32)
                for n in range(1, 32):
                    total = total + mir[n, s].astype(F32)
                p3r[s] = total.astype(BF16)

    @pl.when(jnp.logical_not(late_mirror))
    def _():
        for s in range(2):
            pltpu.make_async_copy(p3r.at[s], p3r.at[s], p3_rs.at[s]).wait()

    br, bl = iota((32, 256), 0), iota((32, 256), 1)
    spread = None
    for s in range(2):
        put = ((bl % 128) == br + NQ * s + SLOT * (bl // 128)) & (br < NQ)
        part = dot(p3r[s], jnp.where(put, 1.0, 0.0).astype(BF16), TN)
        spread = part if spread is None else spread + part
    line = []
    for t in range(plan.slots // 2):
        both = []
        for u in range(2):
            lo = (2 * t + u) * SLOT
            a0 = spread[lo:lo + 32, u * 128:(u + 1) * 128]
            a1 = spread[lo + NQ:lo + NQ + 32, u * 128:(u + 1) * 128]
            both.append(jnp.where(row % 2 == 0, a0, a1))
        line.append(both[0] + both[1])
    swapped = jnp.concatenate(line, axis=1).astype(BF16)
    res = base - dot(swapped, zmat[...], NN)
    for i in range(OW):
        out[i] = res[0:NQ, i * 256:i * 256 + NP * OW]

    for part in range(plan.parts):
        for d in range(2):
            for step in range(4):
                if goes(d, step, part):
                    hop(d, step, part).wait_send()
    swap(yh).wait_send()
    for n in range(plan.paired):
        mate_copy(n).wait_send()

    if plan.direct:
        pltpu.make_async_copy(mir.at[pl.ds(0, 4)], mir.at[pl.ds(0, 4)], m_s).wait()

    @pl.when(home == yh)
    def _():
        pltpu.make_async_copy(msg.at[pl.ds(1, plan.messages - 1)], msg.at[pl.ds(1, plan.messages - 1)], p2_s).wait()

    @pl.when(home != yh)
    def _():
        pltpu.make_async_copy(msg, msg, p2_s).wait()

    for s in range(2):
        @pl.when(jnp.logical_not(late_mirror | ((2 * col + s == row) & (mirror_col == col))))
        def _():
            mirror_copy(s).wait_send()


def call(lanes, cap, slots, collective_id, amps, integral, virt_irrep, occ_irrep):
    plan = Plan(lanes, cap, slots)
    vmem = pl.BlockSpec(memory_space=pltpu.VMEM)
    smem = pl.BlockSpec(memory_space=pltpu.SMEM)
    dma = pltpu.SemaphoreType.DMA
    return pl.pallas_call(
        functools.partial(kernel, plan),
        out_shape=jax.ShapeDtypeStruct((OW, NQ, NP * OW), F32),
        in_specs=[vmem, vmem, vmem, smem, smem],
        out_specs=vmem,
        scratch_shapes=[
            pltpu.VMEM((ZN, plan.count, 16, 128), BF16),
            pltpu.VMEM((YH, plan.count, 16, 128), BF16),
            pltpu.VMEM((plan.rest * 16, plan.wide * 128), F32),
            pltpu.VMEM((plan.group * 256, plan.wide * 128), BF16),
            pltpu.VMEM((plan.group * 256, plan.wide * 128), BF16),
            pltpu.VMEM((5, plan.wide * 128, 512), BF16),
            pltpu.VMEM((48 * plan.full + 16 * plan.rest, 512), F32),
            pltpu.VMEM((ZN, OW * SLOT, plan.depth), BF16),
            pltpu.VMEM((YH, OW * SLOT, plan.depth), BF16),
            pltpu.VMEM((OW * SLOT, 512), F32),
            pltpu.VMEM((plan.paired, 32, YH * plan.msg), F32),
            pltpu.VMEM((plan.paired, 32, YH * plan.msg), BF16),
            pltpu.VMEM((plan.paired, 32, YH * plan.msg), BF16),
            pltpu.VMEM((plan.messages, 32, plan.msg), BF16),
            pltpu.VMEM((32, 32, plan.msg), BF16),
            pltpu.VMEM((plan.msg, OW * 256), BF16),
            pltpu.VMEM((32, plan.msg), BF16),
            pltpu.VMEM((2, 32, plan.msg), BF16),
            dma((8 * plan.parts,)), dma((8 * plan.parts,)), dma, dma, dma((plan.paired,)), dma((plan.paired,)), dma, dma, dma((2,)), dma((2,)),
            pltpu.VMEM((32 if plan.direct else 1, 2, 32, plan.msg), BF16), dma, dma,
            pltpu.SemaphoreType.REGULAR((28,)),
        ],
        name="cycle%d" % lanes,
        compiler_params=pltpu.CompilerParams(
            collective_id=collective_id, has_side_effects=True, vmem_limit_bytes=48 * 2**20),
    )(amps, integral, occ_irrep.reshape(1, NO), occ_irrep, virt_irrep)


TIERS = ((64, 32, 2), (96, 32, 4), (OW * NO, NO, 6))


def shards(amps, integral, virt_irrep, occ_irrep):
    partner = jnp.concatenate([occ_irrep[:OW], jnp.zeros((1,), I32)])
    weight = np.full((NO, OW + 1, 1), 1, np.int32)
    weight[:, OW] = 1 << 10
    weight[:OW, :OW] += 1 << 18
    irreps = jnp.arange(8, dtype=I32)
    hits = (occ_irrep[:, None, None] ^ partner[None, :, None]) == irreps
    sums = jnp.sum(jnp.where(hits, weight, 0), axis=(0, 1))
    need = sums % (1 << 10)
    most = (sums % (1 << 18)) // (1 << 10)
    pairs = (sums // (1 << 18) - jnp.where(irreps == 0, OW, 0)) // 2
    tier = jnp.zeros((8,), I32)
    for lanes, cap, slots in TIERS[:-1]:
        tier = tier + jnp.where((need > lanes) | (most > cap) | (pairs > slots), 1, 0)
    tier = jnp.max(tier)
    calls = [functools.partial(call, lanes, cap, slots, n) for n, (lanes, cap, slots) in enumerate(TIERS)]
    tile = lax.switch(tier, calls, amps.transpose(1, 0, 2), integral, virt_irrep, occ_irrep)
    return tile.transpose(1, 0, 2)


def solution(mesh):
    placed = (P("col", "row", None), P("row", "col", None), P(), P())
    return jax.shard_map(
        shards, mesh=mesh, in_specs=placed, out_specs=P("row", None, "col"), check_vma=False
    )
```

```python
import functools

import jax
import jax.numpy as jnp
import numpy as np
from jax import lax
from jax.experimental import pallas as pl
from jax.experimental.pallas import tpu as pltpu
from jax.sharding import PartitionSpec as P

MESH = pl.DeviceIdType.MESH
F32 = jnp.float32
BF16 = jnp.bfloat16
I32 = jnp.int32

NP = 50
NQ = 25
OW = 4
NO = 64
PAIRS = ((0, 1), (0, 2), (0, 3), (1, 2), (1, 3), (2, 3))
SLOT = 64
ZN = 8
YH = 2


def iota(shape, dim):
    return lax.broadcasted_iota(I32, shape, dim)


def dot(a, b, dims):
    return lax.dot_general(a, b, (dims, ((), ())), preferred_element_type=F32)


class Plan:
    def __init__(self, lanes, cap, slots):
        self.lanes, self.cap, self.slots = lanes, cap, slots
        self.msg = slots * SLOT
        self.parts = 2
        self.near = 2 if slots == 2 else 3
        self.paired = 2 * self.near - 1
        self.messages = 2 * self.paired + 4 * (ZN - self.paired)
        self.direct = slots == 2
        self.group = 128 // cap
        self.full = NQ // self.group
        self.wide = self.group * lanes // 128
        self.last = -(-lanes // 128)
        self.span = self.full * self.wide + self.last
        self.rest = -(-2 * (self.full + 1) // 16)
        self.count = 3 * self.span + self.rest * self.wide
        self.depth = (self.full + 1) * 128


NN = ((1,), (0,))
NT = ((1,), (1,))
TN = ((0,), (0,))


def kernel(plan, amps, integral, occ_row, occ, virt, out, blk, wblk, rest32, st, sw, ex, y32, texp, wall, c32, keep, psend,
           precv, msg, p2r, zmat, tile, p3r, ag_s, ag_r, w_s, w_r, d_s, d_r, p2_s, p2_rs, p3_s, p3_rs, mir, m_s, m_rs, word):
    group, wide, span, full = plan.group, plan.wide, plan.span, plan.full
    dense = plan.lanes == OW * NO
    row = lax.axis_index("row")
    col = lax.axis_index("col")
    core = row % 2
    chip = row // 2
    yh = col // ZN
    z = col % ZN

    right = yh * ZN + (z + 1) % ZN
    left = yh * ZN + (z + ZN - 1) % ZN
    opposite = (1 - yh) * ZN + z
    mate = row + 1 - 2 * core
    home = chip // ZN
    home_z = chip % ZN
    gap = (home_z + ZN - z) % ZN
    late_owner = (gap >= plan.near) & (gap <= ZN - plan.near)
    mirror_col = row // 2

    x, y = row // 8, yh * 4 + chip % 4

    def at_x(d):
        return ((x + 4 + d) % 4 * 8 + row % 8, col)

    def at_y(d):
        to = (y + 8 + d) % 8
        return (x * 8 + to % 4 * 2 + core, to // 4 * ZN + z)

    def at_z(d):
        return (row, yh * ZN + (z + ZN + d) % ZN)

    bar = pltpu.get_barrier_semaphore()
    near = [at(d) for at in (at_x, at_y, at_z) for d in (1, -1)] + [(mate, col)]
    for to in near:
        pl.semaphore_signal(bar, inc=1, device_id=to, device_id_type=MESH)

    rounds = (
        ((at_y, 1), (at_y, -1)), ((at_x, 1), (at_x, -1), (at_y, 2), (at_y, -2)), ((at_y, 3), (at_y, -3)),
        (None,), ((at_z, 1), (at_z, -1)), ((at_z, 2), (at_z, -2)), ((at_z, 1),))

    def tell(n):
        for way, to in enumerate(rounds[n]):
            pl.semaphore_signal(word.at[4 * n + way], inc=1, device_id=(mate, col) if to is None else to[0](to[1]),
                                device_id_type=MESH)

    def hear(n):
        for way in range(len(rounds[n])):
            pl.semaphore_wait(word.at[4 * n + way], 1)

    block_irrep = virt[row // 4]
    lab = occ_row[...]

    def offsets(label):
        counts = [jnp.sum(jnp.where(lab == (label ^ occ[i]), 1.0, 0.0), axis=1, keepdims=True).astype(I32) for i in range(OW)]
        if dense:
            return [jnp.full((1, 1), i * NO, I32) for i in range(OW)], [jnp.full((1, 1), NO, I32)] * OW
        return [sum(counts[:i], jnp.zeros((1, 1), I32)) for i in range(OW)], counts

    def by_window(which, values):
        return jnp.where(which == 0, values[0], jnp.where(which == 1, values[1], jnp.where(which == 2, values[2], values[3])))

    labf = lab.astype(F32)
    r256, l64 = iota((256, NO), 0), iota((256, NO), 1)
    here = virt[col // 2] ^ block_irrep
    here_off, _ = offsets(here)
    pl_lane = iota((1, group * plan.lanes), 1)

    def select(ref, k_of, i_of):
        hk = jnp.sum(jnp.where(l64 == k_of, labf, 0.0), axis=1, keepdims=True)
        k1, i1 = k_of[:, :1], i_of[:, :1]
        hi = by_window(i1, [occ[i] for i in range(OW)])
        if dense:
            place = k1
        else:
            same = (labf == hk) & (l64 < k_of)
            place = jnp.sum(jnp.where(same, 1.0, 0.0), axis=1, keepdims=True).astype(I32)
        key = jnp.where((hk.astype(I32) ^ hi) == here, by_window(i1, here_off) + place, -1)
        for g in range(group):
            hit = (key == pl_lane % plan.lanes) & (pl_lane // plan.lanes == g)
            ref[g * 256:(g + 1) * 256, :] = jnp.where(hit, 1.0, 0.0).astype(BF16)

    def pack(planes, sel, dst):
        for q in range(full + 1):
            cs = range(q * group, min(NQ, (q + 1) * group))
            many = wide if q < full else plan.last
            x = jnp.concatenate([planes[c] for c in cs], axis=1)
            y = dot(x, sel[0:len(cs) * 256, 0:many * 128], NN)
            for r in range(3):
                for t in range(many):
                    dst[r * span + q * wide + t] = y[r * 16:(r + 1) * 16, t * 128:(t + 1) * 128].astype(BF16)
            rest32[2 * q:2 * q + 2, 0:many * 128] = y[48:50, :]
        for r in range(plan.rest):
            for t in range(wide):
                dst[3 * span + r * wide + t] = rest32[r * 16:(r + 1) * 16, t * 128:(t + 1) * 128].astype(BF16)

    def expand(src, sel, dst):
        lines = [jnp.concatenate([src[r * span + q * wide + t] for t in range(wide)], axis=1)
                 for q in range(full) for r in range(3)]
        lines += [jnp.concatenate([src[3 * span + r * wide + t] for t in range(wide)], axis=1) for r in range(plan.rest)]
        tall = 48 * full
        y32[0:tall + 16 * plan.rest, :] = dot(jnp.concatenate(lines, axis=0), sel[...], NN)
        x = jnp.concatenate([jnp.concatenate([src[r * span + full * wide + t] for t in range(plan.last)], axis=1)
                             for r in range(3)], axis=0)
        z6 = dot(x, sel[0:plan.last * 128, :], NN)
        for q in range(full + 1):
            for i in range(OW):
                lanes = slice(i * 128, (i + 1) * 128)
                main = y32[q * 48:(q + 1) * 48, lanes] if q < full else z6[:, lanes]
                dst[i * SLOT:i * SLOT + 48, q * 128:(q + 1) * 128] = main.astype(BF16)
                dst[i * SLOT + 48:i * SLOT + 50, q * 128:(q + 1) * 128] = (
                    y32[tall + 2 * q:tall + 2 * q + 2, lanes].astype(BF16))

    rest32[...] = jnp.zeros(rest32.shape, F32)
    select(st, r256 % NO, r256 // NO)
    pack(amps, st, blk.at[z])

    pl.semaphore_wait(bar, len(near))

    edges = [plan.count * n // plan.parts for n in range(plan.parts + 1)]

    def goes(direction, step, part):
        return step < 3 or (part < plan.parts // 2) == (direction == 0)

    def moved(direction, step, part, src):
        n = (direction * 4 + step) * plan.parts + part
        ref = blk.at[src, pl.ds(edges[part], edges[part + 1] - edges[part])]
        return pltpu.make_async_remote_copy(
            src_ref=ref, dst_ref=ref, send_sem=ag_s.at[n], recv_sem=ag_r.at[n],
            device_id=(row, right if direction == 0 else left), device_id_type=MESH)

    def hop(direction, step, part):
        return moved(direction, step, part, (z + ZN - step) % ZN if direction == 0 else (z + step) % ZN)

    def arrival(direction, step, part):
        return moved(direction, step, part, (z + ZN - step - 1) % ZN if direction == 0 else (z + step + 1) % ZN)

    for part in range(plan.parts):
        for d in range(2):
            hop(d, 0, part).start()

    tell(0)
    select(sw, r256 // OW, r256 % OW)
    pack(integral, sw, wblk.at[yh])
    hear(0)
    tell(1)

    def swap(which):
        return pltpu.make_async_remote_copy(
            src_ref=wblk.at[which], dst_ref=wblk.at[which], send_sem=w_s, recv_sem=w_r, device_id=(row, opposite),
            device_id_type=MESH)

    er = iota((group * plan.lanes, 1), 0)
    el = iota((1, 512), 1)
    e_i, e_g, e_m = el // 128, (el % 128) // plan.cap, el % plan.cap
    for n in range(5):
        label = block_irrep ^ (virt[yh * 4 + n] if n < 4 else virt[(1 - yh) * 4 + z // 2])
        off, counts = offsets(label)
        key = jnp.where(e_m < by_window(e_i, counts), by_window(e_i, off) + e_m, -1)
        hit = (er % plan.lanes == key) & (er // plan.lanes == e_g)
        ex[n] = jnp.where(hit, 1.0, 0.0).astype(BF16)

    def slots(label):
        alive = [(occ[i] ^ occ[j]) == label for i, j in PAIRS]
        if plan.slots == len(PAIRS):
            return [[alive[p] if p == n else None for p in range(len(PAIRS))] for n in range(plan.slots)]
        ones = [jnp.where(a, 1, 0) for a in alive]
        return [[alive[p] & (sum(ones[:p], 0) == n) if p >= n else None for p in range(len(PAIRS))]
                for n in range(plan.slots)]

    def spread_matrix():
        zr, zl = iota((plan.msg, OW * 256), 0), iota((plan.msg, OW * 256), 1)
        zr1 = zr[:, :1]
        first = second = jnp.full((plan.msg, 1), -1, I32)
        for n, taken in enumerate(slots(here)):
            for p, (i, j) in enumerate(PAIRS):
                if taken[p] is not None:
                    it = (zr1 // SLOT == n) & taken[p]
                    first, second = jnp.where(it, i, first), jnp.where(it, j, second)
        zb = zr1 % SLOT
        zl1 = zl[:1]
        zi, zt = zl1 // 256, zl1 % 256
        in_b = (zt // OW == zb) & (zb < NP)
        plus = in_b & (zi == first) & (zt % OW == second)
        minus = in_b & (zi == second) & (zt % OW == first)
        zmat[...] = (jnp.where(plus, 1.0, 0.0) - jnp.where(minus, 1.0, 0.0)).astype(BF16)

    low = iota((32, 128), 1) < SLOT

    def source(n):
        return (z + ZN + n // 2 - n % 2 * (2 * (n // 2) + 1)) % ZN

    def each(first, many, *steps):
        def body(k, carry):
            for step in steps:
                step(first + k, first)
            return carry

        lax.fori_loop(0, many, body, 0)

    def unpack(n, first=0):
        za = source(n)
        expand(blk.at[za], ex.at[za // 2], texp.at[n])

    def mate_copy(n):
        return pltpu.make_async_remote_copy(
            src_ref=psend.at[n], dst_ref=precv.at[n], send_sem=d_s.at[n], recv_sem=d_r.at[n], device_id=(mate, col),
            device_id_type=MESH)

    def differences(n):
        za = source(n)
        for h in range(YH):
            c32[:, h * 256:(h + 1) * 256] = dot(texp[n], wall[h], NT)
        la = virt[(yh * ZN + za) // 2]
        taken_by = [slots(la ^ virt[(h * ZN + z) // 2]) for h in range(YH)]
        halves = []
        for half in range(2):
            line = []
            for h in range(YH):
                values = []
                for i, j in PAIRS:

                    def piece(r, q):
                        start = SLOT * r + NQ * half
                        v = c32[start:start + 32, h * 256 + (q // 2) * 128:h * 256 + (q // 2) * 128 + 128]
                        return v if q % 2 == 0 else pltpu.roll(v, SLOT, axis=1)

                    values.append(piece(i, j) - piece(j, i))
                pieces = []
                for n, taken in enumerate(taken_by[h]):
                    v = sum(values[p] * jnp.where(t, 1.0, 0.0) for p, t in enumerate(taken) if t is not None)
                    pieces.append(v if n % 2 == 0 else pltpu.roll(v, SLOT, axis=1))
                for n in range(0, plan.slots, 2):
                    line.append(jnp.where(low, pieces[n], pieces[n + 1]))
            halves.append(jnp.concatenate(line, axis=1))
        return halves

    def compute(n):
        halves = differences(n)
        keep[n] = jnp.where(core == 0, halves[0], halves[1])
        psend[n] = jnp.where(core == 0, halves[1], halves[0]).astype(BF16)
        mate_copy(n).start()

    def deliver(m, to_row, h, place):
        mine = (to_row == row) & (yh == h)

        @pl.when(jnp.logical_not(mine))
        def _():
            pltpu.make_async_remote_copy(
                src_ref=msg.at[m], dst_ref=p2r.at[place], send_sem=p2_s, recv_sem=p2_rs,
                device_id=(to_row, h * ZN + z), device_id_type=MESH).start()

        @pl.when(mine)
        def _():
            pltpu.make_async_copy(msg.at[m], p2r.at[place], p2_rs).start()

    def finish(n):
        za = source(n)
        mate_copy(n).wait_recv()
        total = (keep[n] + precv[n].astype(F32)).astype(BF16)
        for h in range(YH):
            msg[2 * n + h] = total[:, h * plan.msg:(h + 1) * plan.msg]
            deliver(2 * n + h, 2 * (yh * ZN + za) + core, h, chip)

    def spread_out(n, last):
        halves = differences(n)
        za = source(n)
        first = 2 * plan.paired + 4 * (n - plan.paired)
        for h in range(YH):
            m = first + 2 * h
            for half in range(2):
                msg[m + half] = halves[half][:, h * plan.msg:(h + 1) * plan.msg].astype(BF16)
            if plan.direct and last:
                for half in range(2):
                    pltpu.make_async_remote_copy(
                        src_ref=msg.at[pl.ds(m, 2)], dst_ref=mir.at[row], send_sem=m_s, recv_sem=m_rs,
                        device_id=(2 * (h * ZN + z) + half, yh * ZN + za), device_id_type=MESH).start()
            for half in range(2):
                deliver(m + half, 2 * (yh * ZN + za) + half, h, row)

    def work(n, first=0):
        if first < plan.paired:
            compute(n)
        else:
            spread_out(n, first == 7)

    def forward(step):
        for part in range(plan.parts):
            for d in range(2):
                arrival(d, step - 1, part).wait_recv()
                if goes(d, step, part):
                    hop(d, step, part).start()

    hear(1)
    swap(yh).start()
    tell(2)
    forward(1)
    texp[...] = jnp.zeros(texp.shape, BF16)
    wall[...] = jnp.zeros(wall.shape, BF16)
    expand(wblk.at[yh], ex.at[z // 2], wall.at[yh])
    hear(2)
    tell(3)
    each(0, 3, unpack)
    forward(2)
    hear(3)
    tell(4)
    spread_matrix()
    each(3, 2, unpack)
    swap(1 - yh).wait_recv()
    expand(wblk.at[1 - yh], ex.at[4], wall.at[1 - yh])
    each(0, 3, work)
    forward(3)
    hear(4)
    tell(5)
    each(3, 2, work)
    for n in range(min(3, plan.paired)):
        finish(n)
    each(5, 2, unpack, work)
    for n in range(3, plan.paired):
        finish(n)
    hear(5)
    tell(6)
    hear(6)
    for part in range(plan.parts):
        for d in range(2):
            if goes(d, 3, part):
                arrival(d, 3, part).wait_recv()
    unpack(7)
    work(7, 7)

    def add_up(many):
        pltpu.make_async_copy(p2r.at[pl.ds(0, many)], p2r.at[pl.ds(0, many)], p2_rs).wait()
        total = p2r[0].astype(F32)
        for n in range(1, many):
            total = total + p2r[n].astype(F32)
        tile[...] = total.astype(BF16)

    @pl.when(late_owner)
    def _():
        add_up(32)

    @pl.when(jnp.logical_not(late_owner))
    def _():
        add_up(16)

    def mirror_copy(s):
        return pltpu.make_async_remote_copy(
            src_ref=tile, dst_ref=p3r.at[row % 2], send_sem=p3_s.at[s], recv_sem=p3_rs.at[row % 2],
            device_id=(2 * col + s, mirror_col), device_id_type=MESH)

    late_mirror = (gap == 4) if plan.direct else (gap < 0)

    @pl.when(jnp.logical_not(late_mirror))
    def _():
        for s in range(2):
            self_mirror = (2 * col + s == row) & (mirror_col == col)

            @pl.when(jnp.logical_not(self_mirror))
            def _():
                mirror_copy(s).start()

            @pl.when(self_mirror)
            def _():
                pltpu.make_async_copy(tile, p3r.at[s], p3_rs.at[s]).start()

    base = dot(tile[...], zmat[...], NN)

    if plan.direct:
        @pl.when(late_mirror)
        def _():
            pltpu.make_async_copy(mir, mir, m_rs).wait()
            for s in range(2):
                total = mir[0, s].astype(F32)
                for n in range(1, 32):
                    total = total + mir[n, s].astype(F32)
                p3r[s] = total.astype(BF16)

    @pl.when(jnp.logical_not(late_mirror))
    def _():
        for s in range(2):
            pltpu.make_async_copy(p3r.at[s], p3r.at[s], p3_rs.at[s]).wait()

    br, bl = iota((32, 256), 0), iota((32, 256), 1)
    spread = None
    for s in range(2):
        put = ((bl % 128) == br + NQ * s + SLOT * (bl // 128)) & (br < NQ)
        part = dot(p3r[s], jnp.where(put, 1.0, 0.0).astype(BF16), TN)
        spread = part if spread is None else spread + part
    line = []
    for t in range(plan.slots // 2):
        both = []
        for u in range(2):
            lo = (2 * t + u) * SLOT
            a0 = spread[lo:lo + 32, u * 128:(u + 1) * 128]
            a1 = spread[lo + NQ:lo + NQ + 32, u * 128:(u + 1) * 128]
            both.append(jnp.where(row % 2 == 0, a0, a1))
        line.append(both[0] + both[1])
    swapped = jnp.concatenate(line, axis=1).astype(BF16)
    res = base - dot(swapped, zmat[...], NN)
    for i in range(OW):
        out[i] = res[0:NQ, i * 256:i * 256 + NP * OW]

    for part in range(plan.parts):
        for d in range(2):
            for step in range(4):
                if goes(d, step, part):
                    hop(d, step, part).wait_send()
    swap(yh).wait_send()
    for n in range(plan.paired):
        mate_copy(n).wait_send()

    if plan.direct:
        pltpu.make_async_copy(mir.at[pl.ds(0, 4)], mir.at[pl.ds(0, 4)], m_s).wait()

    @pl.when(home == yh)
    def _():
        pltpu.make_async_copy(msg.at[pl.ds(1, plan.messages - 1)], msg.at[pl.ds(1, plan.messages - 1)], p2_s).wait()

    @pl.when(home != yh)
    def _():
        pltpu.make_async_copy(msg, msg, p2_s).wait()

    for s in range(2):
        @pl.when(jnp.logical_not(late_mirror | ((2 * col + s == row) & (mirror_col == col))))
        def _():
            mirror_copy(s).wait_send()


def call(lanes, cap, slots, collective_id, amps, integral, virt_irrep, occ_irrep):
    plan = Plan(lanes, cap, slots)
    vmem = pl.BlockSpec(memory_space=pltpu.VMEM)
    smem = pl.BlockSpec(memory_space=pltpu.SMEM)
    dma = pltpu.SemaphoreType.DMA
    return pl.pallas_call(
        functools.partial(kernel, plan),
        out_shape=jax.ShapeDtypeStruct((OW, NQ, NP * OW), F32),
        in_specs=[vmem, vmem, vmem, smem, smem],
        out_specs=vmem,
        scratch_shapes=[
            pltpu.VMEM((ZN, plan.count, 16, 128), BF16),
            pltpu.VMEM((YH, plan.count, 16, 128), BF16),
            pltpu.VMEM((plan.rest * 16, plan.wide * 128), F32),
            pltpu.VMEM((plan.group * 256, plan.wide * 128), BF16),
            pltpu.VMEM((plan.group * 256, plan.wide * 128), BF16),
            pltpu.VMEM((5, plan.wide * 128, 512), BF16),
            pltpu.VMEM((48 * plan.full + 16 * plan.rest, 512), F32),
            pltpu.VMEM((ZN, OW * SLOT, plan.depth), BF16),
            pltpu.VMEM((YH, OW * SLOT, plan.depth), BF16),
            pltpu.VMEM((OW * SLOT, 512), F32),
            pltpu.VMEM((plan.paired, 32, YH * plan.msg), F32),
            pltpu.VMEM((plan.paired, 32, YH * plan.msg), BF16),
            pltpu.VMEM((plan.paired, 32, YH * plan.msg), BF16),
            pltpu.VMEM((plan.messages, 32, plan.msg), BF16),
            pltpu.VMEM((32, 32, plan.msg), BF16),
            pltpu.VMEM((plan.msg, OW * 256), BF16),
            pltpu.VMEM((32, plan.msg), BF16),
            pltpu.VMEM((2, 32, plan.msg), BF16),
            dma((8 * plan.parts,)), dma((8 * plan.parts,)), dma, dma, dma((plan.paired,)), dma((plan.paired,)), dma, dma, dma((2,)), dma((2,)),
            pltpu.VMEM((32 if plan.direct else 1, 2, 32, plan.msg), BF16), dma, dma,
            pltpu.SemaphoreType.REGULAR((28,)),
        ],
        name="cycle%d" % lanes,
        compiler_params=pltpu.CompilerParams(
            collective_id=collective_id, has_side_effects=True, vmem_limit_bytes=48 * 2**20),
    )(amps, integral, occ_irrep.reshape(1, NO), occ_irrep, virt_irrep)


TIERS = ((64, 32, 2), (96, 32, 4), (128, 32, 6), (OW * NO, NO, 6))


def shards(amps, integral, virt_irrep, occ_irrep):
    partner = jnp.concatenate([occ_irrep[:OW], jnp.zeros((1,), I32)])
    weight = np.full((NO, OW + 1, 1), 1, np.int32)
    weight[:, OW] = 1 << 10
    weight[:OW, :OW] += 1 << 18
    irreps = jnp.arange(8, dtype=I32)
    hits = (occ_irrep[:, None, None] ^ partner[None, :, None]) == irreps
    sums = jnp.sum(jnp.where(hits, weight, 0), axis=(0, 1))
    need = sums % (1 << 10)
    most = (sums % (1 << 18)) // (1 << 10)
    pairs = (sums // (1 << 18) - jnp.where(irreps == 0, OW, 0)) // 2
    tier = jnp.zeros((8,), I32)
    for lanes, cap, slots in TIERS[:-1]:
        tier = tier + jnp.where((need > lanes) | (most > cap) | (pairs > slots), 1, 0)
    tier = jnp.max(tier)
    calls = [functools.partial(call, lanes, cap, slots, n) for n, (lanes, cap, slots) in enumerate(TIERS)]
    tile = lax.switch(tier, calls, amps.transpose(1, 0, 2), integral, virt_irrep, occ_irrep)
    return tile.transpose(1, 0, 2)


def solution(mesh):
    placed = (P("col", "row", None), P("row", "col", None), P(), P())
    return jax.shard_map(
        shards, mesh=mesh, in_specs=placed, out_specs=P("row", None, "col"), check_vma=False
    )
```
